32 devices in a mesh: groups: 2 (over x), cells: 16 (over z, y, core).
Axes of the slice: x: 2, y: 2, z: 4, core: 2. Of those that a mesh axis runs over, the one named last changes fastest.
Arguments:
- jacobian: bfloat16 [7, 9, 128, 32, 256], P(None, None, ('groups', 'cells')), parts along dimension 2, may hold values from -1.625 to 12, as said below
- right_side: float32 [3, 128, 32, 256], P(None, ('groups', 'cells')), parts along dimension 1, may hold values from -108 to 108
- scales: float32 [3, 128, 32, 256], P(None, ('groups', 'cells')), parts along dimension 1, may hold values from 0.5 to 2
- weights: float32 [3, 128, 32, 256], P(None, ('groups', 'cells')), parts along dimension 1, may hold values from 0.5 to 2
- aggregate_of: int32 [128, 32, 256], P(('groups', 'cells')), parts along dimension 0, may hold values from 0 to 255, as said below
Outputs:
- solution: float32 [3, 128, 32, 256], P(None, ('groups', 'cells')), parts along dimension 1
- residual: float32 [3, 128, 32, 256], P(None, ('groups', 'cells')), parts along dimension 1
The draws below stay inside these ranges and needn't reach their ends.
There are 2 independent parts, one for each index of `groups`. The reference program is written for one: setup_inputs(seed, part) draws one part's arguments, and reference() takes and returns one part's arrays. A program takes and returns all parts, laid end to end along the dimension named above; each array names one. Nothing has to cross between parts.
Inputs may be any that keep to these rules, and one draw needn't show every extreme that they name: In every block jacobian[k] the first column's entries of the neighbours (k >= 1) are negative, and for each row r the entry jacobian[0, 3 r] exceeds the sum of the magnitudes of jacobian[k, 3 r] over k = 1..6; each cell's own 3 x 3 block is diagonally dominant by rows. `aggregate_of`: every aggregate of 0 to 255 holds cells in every slab. Aggregate a covers base box row a // 32 and column a % 32; the cell in grid row y and column x belongs to an aggregate whose box row is one of (y - 1) // 4, y // 4, (y + 1) // 4 and whose box column is one of (x - 1) // 8, x // 8, (x + 1) // 8, within the grid.
All inputs are finite; a program needn't handle non-finite values.
Results may differ from the reference program's by a relative error of at most 0.0003.
Values sent between devices are 32-bit elements; how exact they have to be, the bound alone decides.
A program may use at most 192 MiB of HBM per device.

```python
import math
import jax
import jax.numpy as jnp
from jax import lax

LZ = 4
GY = 32
GX = 256
AY = 4
AX = 8
NAGG = 256
NZ = 64
N_CELLS = 16


def draw_jacobian(key, part):
    key = jax.random.fold_in(key, 11)
    sub_keys = jax.random.split(key, 5)
    grid_shape = (NZ, GY, GX)
    outer_col = -jax.random.uniform(sub_keys[0], (6, 3) + grid_shape, jnp.float32, 0.4, 1.6)
    margin = jax.random.uniform(sub_keys[1], (3,) + grid_shape, jnp.float32, 0.1, 0.6)
    row_factor = jnp.array([1.0, 0.3, 0.3], jnp.float32).reshape(3, 1, 1, 1)
    first_outer = outer_col * row_factor
    first_self = (jnp.sum(-outer_col, axis=0) + margin) * row_factor
    leading = jax.random.uniform(sub_keys[2], (2,) + grid_shape, jnp.float32, 8.0, 12.0)
    coupling = jax.random.uniform(sub_keys[3], (4,) + grid_shape, jnp.float32, -0.5, 0.5)
    side_cols = jax.random.uniform(sub_keys[4], (6, 3, 2) + grid_shape, jnp.float32, -1.0, 0.3)
    self_block = jnp.stack([first_self[0], coupling[0], coupling[1], first_self[1], leading[0], coupling[2], first_self[2], coupling[3], leading[1]])
    blocks = [self_block]
    for way_index in range(6):
        entries = []
        for row_index in range(3):
            entries = entries + [first_outer[way_index, row_index], side_cols[way_index, row_index, 0], side_cols[way_index, row_index, 1]]
        blocks.append(jnp.stack(entries))
    return jnp.stack(blocks).astype(jnp.bfloat16)


def draw_right_side(key, part):
    key = jax.random.fold_in(key, 12)
    sub_keys = jax.random.split(key, 3)
    layers = jnp.arange(NZ, dtype=jnp.float32)
    rising = (1.0 + 2.0 * layers / max(NZ - 1, 1)).reshape(1, NZ, 1, 1)
    row_scale = jnp.exp(jax.random.uniform(sub_keys[0], (GY,), jnp.float32, math.log(0.3), math.log(3.0))).reshape(1, 1, GY, 1)
    column_scale = jnp.exp(jax.random.uniform(sub_keys[1], (GX,), jnp.float32, math.log(0.3), math.log(3.0))).reshape(1, 1, 1, GX)
    values = jax.random.truncated_normal(sub_keys[2], -4.0, 4.0, (3, NZ, GY, GX), jnp.float32)
    return values * rising * row_scale * column_scale


def draw_aggregate_of(key, part):
    key = jax.random.fold_in(key, 13)
    sub_keys = jax.random.split(key, 2)
    grid_shape = (NZ, GY, GX)
    row_step = jax.random.randint(sub_keys[0], grid_shape, -1, 2)
    col_step = jax.random.randint(sub_keys[1], grid_shape, -1, 2)
    rows_at = jnp.clip(jnp.arange(GY).reshape(1, GY, 1) + row_step, 0, GY - 1)
    cols_at = jnp.clip(jnp.arange(GX).reshape(1, 1, GX) + col_step, 0, GX - 1)
    return (rows_at // AY * (GX // AX) + cols_at // AX).astype(jnp.int32)


def block_levels(own_key, shape, cuts, low, largest):
    level, own = 1.0, jax.random.fold_in(own_key, 6)
    for dim, blocks in cuts:
        steps = jnp.exp(jax.random.uniform(jax.random.fold_in(own, dim), (blocks,), jnp.float32, low / len(cuts), largest / len(cuts)))
        level = level * jnp.repeat(steps, shape[dim] // blocks).reshape([-1 if axis == dim else 1 for axis in range(len(shape))])
    return level


def setup_inputs(seed: int = 0, part: int = 0) -> dict:
    key_of = jax.random.split(jax.random.key(seed), 6)
    part_splits = jax.random.split(jax.random.fold_in(key_of[5], part), 6)
    return {
        "jacobian": draw_jacobian(jax.random.fold_in(jax.random.fold_in(key_of[5], part), 71), part),
        "right_side": draw_right_side(jax.random.fold_in(jax.random.fold_in(key_of[5], part), 71), part),
        "scales": jnp.clip(jnp.exp(math.log(2.0) - 1.3862944 * jax.random.uniform(part_splits[2], (3, NZ, GY, GX), jnp.float32) ** block_levels(part_splits[2], (3, NZ, GY, GX), ((1, 16),), -0.2, 0.2)), 0.5, 2.0),
        "weights": jnp.clip(jnp.exp(math.log(2.0) - 1.3862944 * jax.random.uniform(part_splits[3], (3, NZ, GY, GX), jnp.float32) ** block_levels(part_splits[3], (3, NZ, GY, GX), ((1, 16),), -0.2, 0.2)), 0.5, 2.0),
        "aggregate_of": draw_aggregate_of(jax.random.fold_in(jax.random.fold_in(key_of[5], part), 71), part),
    }


DAMPING = 2.0 / 3.0
PRECISE = lax.Precision.HIGHEST

def neighbour_views(padded):
    return [padded[..., 1:-1, 1:-1, 1:-1], padded[..., :-2, 1:-1, 1:-1], padded[..., 2:, 1:-1, 1:-1], padded[..., 1:-1, :-2, 1:-1], padded[..., 1:-1, 2:, 1:-1], padded[..., 1:-1, 1:-1, :-2], padded[..., 1:-1, 1:-1, 2:]]

def stencil_sum(pressure_coef, padded):
    shifted = neighbour_views(padded)
    summed = pressure_coef[0] * shifted[0]
    for way_index in range(1, 7):
        summed = summed + pressure_coef[way_index] * shifted[way_index]
    return summed

def block_product(jacobian, scales, padded):
    shifted = neighbour_views(padded)
    rows_out = []
    for row_index in range(3):
        summed = jnp.zeros(shifted[0].shape[1:], jnp.float32)
        for way_index in range(7):
            for comp_index in range(3):
                block_entry = jacobian[way_index, 3 * row_index + comp_index].astype(jnp.float32)
                summed = summed + block_entry * shifted[way_index][comp_index]
        rows_out.append(scales[row_index] * summed)
    return jnp.stack(rows_out)

def pressure_terms(jacobian, scales, weights):
    coef_list = []
    for way_index in range(7):
        summed = weights[0] * scales[0] * jacobian[way_index, 0].astype(jnp.float32)
        for row_index in range(1, 3):
            summed = summed + weights[row_index] * scales[row_index] * jacobian[way_index, 3 * row_index].astype(jnp.float32)
        coef_list.append(summed)
    return jnp.stack(coef_list)

def block_solve(jacobian, values_in):
    mat = [jacobian[0, idx_entry].astype(jnp.float32) for idx_entry in range(9)]
    co_aa = mat[4] * mat[8] - mat[5] * mat[7]
    co_ab = -(mat[3] * mat[8] - mat[5] * mat[6])
    co_ac = mat[3] * mat[7] - mat[4] * mat[6]
    co_ba = -(mat[1] * mat[8] - mat[2] * mat[7])
    co_bb = mat[0] * mat[8] - mat[2] * mat[6]
    co_bc = -(mat[0] * mat[7] - mat[1] * mat[6])
    co_ca = mat[1] * mat[5] - mat[2] * mat[4]
    co_cb = -(mat[0] * mat[5] - mat[2] * mat[3])
    co_cc = mat[0] * mat[4] - mat[1] * mat[3]
    determinant = mat[0] * co_aa + mat[1] * co_ab + mat[2] * co_ac
    first_out = (co_aa * values_in[0] + co_ba * values_in[1] + co_ca * values_in[2]) / determinant
    second_out = (co_ab * values_in[0] + co_bb * values_in[1] + co_cb * values_in[2]) / determinant
    third_out = (co_ac * values_in[0] + co_bc * values_in[1] + co_cc * values_in[2]) / determinant
    return jnp.stack([first_out, second_out, third_out])

def slab_tiles(aggregate_ids, pressure_coef, below_ids, above_ids):
    pairs = [(aggregate_ids, aggregate_ids, pressure_coef[0]), (aggregate_ids[1:], aggregate_ids[:-1], pressure_coef[1][1:]), (aggregate_ids[:-1], aggregate_ids[1:], pressure_coef[2][:-1]), (aggregate_ids[:, 1:], aggregate_ids[:, :-1], pressure_coef[3][:, 1:]), (aggregate_ids[:, :-1], aggregate_ids[:, 1:], pressure_coef[4][:, :-1]), (aggregate_ids[:, :, 1:], aggregate_ids[:, :, :-1], pressure_coef[5][:, :, 1:]), (aggregate_ids[:, :, :-1], aggregate_ids[:, :, 1:], pressure_coef[6][:, :, :-1])]
    self_flat = jnp.zeros((NAGG * NAGG,), jnp.float32)
    for row_ids, col_ids, coef_vals in pairs:
        self_flat = self_flat.at[(row_ids * NAGG + col_ids).reshape(-1)].add(coef_vals.reshape(-1))
    lower_vals = jnp.where(below_ids > 0, pressure_coef[1][0], 0.0)
    lower_cols = jnp.maximum(below_ids - 1, 0)
    lower_flat = jnp.zeros((NAGG * NAGG,), jnp.float32).at[(aggregate_ids[0] * NAGG + lower_cols).reshape(-1)].add(lower_vals.reshape(-1))
    upper_vals = jnp.where(above_ids > 0, pressure_coef[2][-1], 0.0)
    upper_cols = jnp.maximum(above_ids - 1, 0)
    upper_flat = jnp.zeros((NAGG * NAGG,), jnp.float32).at[(aggregate_ids[-1] * NAGG + upper_cols).reshape(-1)].add(upper_vals.reshape(-1))
    return (self_flat.reshape(NAGG, NAGG), lower_flat.reshape(NAGG, NAGG), upper_flat.reshape(NAGG, NAGG))

def coarse_global(self_tile, lower_tile, upper_tile, coarse):
    empty_row = jnp.zeros((1, coarse.shape[1]), jnp.float32)
    from_below = jnp.concatenate([empty_row, coarse[:-1]], 0)
    from_above = jnp.concatenate([coarse[1:], empty_row], 0)
    summed = jnp.einsum('sij,sj->si', self_tile, coarse, precision=PRECISE)
    summed = summed + jnp.einsum('sij,sj->si', lower_tile, from_below, precision=PRECISE)
    return summed + jnp.einsum('sij,sj->si', upper_tile, from_above, precision=PRECISE)

def reference(jacobian, right_side, scales, weights, aggregate_of):
    slabs = N_CELLS
    pressure_coef = pressure_terms(jacobian, scales, weights)

    def pressure_apply(values_in):
        return stencil_sum(pressure_coef, jnp.pad(values_in, 1))

    def field_apply(values_in):
        return block_product(jacobian, scales, jnp.pad(values_in, ((0, 0), (1, 1), (1, 1), (1, 1))))
    slab_ids = aggregate_of.reshape(slabs, LZ, GY, GX)
    slab_coef = pressure_coef.reshape(7, slabs, LZ, GY, GX).transpose(1, 0, 2, 3, 4)
    empty_ids = jnp.zeros((1, GY, GX), jnp.int32)
    below_all = jnp.concatenate([empty_ids, slab_ids[:-1, -1] + 1], 0).astype(jnp.int32)
    above_all = jnp.concatenate([slab_ids[1:, 0] + 1, empty_ids], 0).astype(jnp.int32)
    self_tile, lower_tile, upper_tile = jax.vmap(slab_tiles)(slab_ids, slab_coef, below_all, above_all)
    coarse_diag = jnp.diagonal(self_tile, axis1=1, axis2=2)
    main_diag = lax.optimization_barrier(jnp.sum(self_tile, axis=(1, 2)))
    lower_diag = lax.optimization_barrier(jnp.sum(lower_tile, axis=(1, 2)))
    upper_diag = lax.optimization_barrier(jnp.sum(upper_tile, axis=(1, 2)))
    side_norm = jnp.sqrt(jnp.sum(right_side * right_side) + 1e-06)
    krylov_basis = right_side / side_norm
    restricted = weights[0] * krylov_basis[0] + weights[1] * krylov_basis[1] + weights[2] * krylov_basis[2]
    diag_fine = pressure_coef[0]
    first_iterate = DAMPING * restricted / diag_fine
    second_iterate = first_iterate + DAMPING * (restricted - pressure_apply(first_iterate)) / diag_fine
    fine_residual = restricted - pressure_apply(second_iterate)
    slab_index = jnp.arange(slabs, dtype=jnp.int32).reshape(slabs, 1, 1, 1)
    coarse_rhs = jnp.zeros((slabs, NAGG), jnp.float32).at[jnp.broadcast_to(slab_index, slab_ids.shape), slab_ids].add(fine_residual.reshape(slabs, LZ, GY, GX))
    coarse_first = DAMPING * coarse_rhs / coarse_diag
    coarse_residual = coarse_rhs - coarse_global(self_tile, lower_tile, upper_tile, coarse_first)
    slab_residual = lax.optimization_barrier(jnp.sum(coarse_residual, axis=1))
    slab_fix = lax.linalg.tridiagonal_solve(lower_diag, main_diag, upper_diag, slab_residual[:, None])[:, 0]
    coarse_second = coarse_first + slab_fix[:, None]
    coarse_third = coarse_second + DAMPING * (coarse_rhs - coarse_global(self_tile, lower_tile, upper_tile, coarse_second)) / coarse_diag
    lifted = jnp.take_along_axis(coarse_third, slab_ids.reshape(slabs, -1), axis=1).reshape(NZ, GY, GX)
    third_iterate = second_iterate + lifted - DAMPING * pressure_apply(lifted) / diag_fine
    pressure_fix = third_iterate + DAMPING * (restricted - pressure_apply(third_iterate)) / diag_fine
    zero_field = jnp.zeros_like(pressure_fix)
    first_section = jnp.stack([pressure_fix, zero_field, zero_field])
    second_rhs = krylov_basis - field_apply(first_section)
    direction = first_section + block_solve(jacobian, second_rhs / scales)
    image = field_apply(direction)
    along_basis = jnp.sum(image * krylov_basis)
    orthogonal = image - along_basis * krylov_basis
    leftover = jnp.sum(orthogonal * orthogonal)
    step_size = side_norm * along_basis / (along_basis * along_basis + leftover)
    return (step_size * direction, right_side - step_size * image)
```

```python
import functools

import jax
import jax.numpy as jnp
from jax import lax
from jax.experimental import pallas as pl
from jax.experimental.pallas import tpu as pltpu
from jax.sharding import PartitionSpec as P

AY = 4
AX = 8
DAMPING = 2.0 / 3.0
LIFT = 1024.0
F32 = jnp.float32
BF16 = jnp.bfloat16


def split_rows(x):
    hi = x.astype(BF16)
    lo = (x - hi.astype(F32)).astype(BF16)
    return jnp.concatenate([hi, lo], axis=0)


def other_box(place, width):
    part = place % width
    own = place // width
    return jnp.where(part == 0, own - 1, jnp.where(part == width - 1, own + 1, -9))


def kernel(
    n, lz, gy, gx,
    jac_hbm, side_hbm, scal_hbm, wei_hbm, ids_hbm,
    dir_hbm, img_hbm, tot_ref,
    jac, side, scal, wei, ids,
    pc, wd, rest, binv, zed, dout, iout,
    f1, f2, cf, lf, t3, pf, dr, c1, c2,
    mask, gidx, sx, sy, inv, shv,
    g0, g4, g9, g0s, g4s, g9s,
    lsem, osem, hs, hr, gs, gr,
):
    me = lax.axis_index("cells")
    has_low = me > 0
    has_high = me < n - 1
    low_id = jnp.maximum(me - 1, 0)
    high_id = jnp.minimum(me + 1, n - 1)
    top = lz - 1
    across = gx // AX
    half = gx // 2
    tiles = gy // 8

    barrier = pltpu.get_barrier_semaphore()

    @pl.loop(1, n)
    def _(step):
        pl.semaphore_signal(
            barrier, inc=1, device_id={"cells": lax.rem(me + step, n)},
            device_id_type=pl.DeviceIdType.MESH,
        )

    loads = []

    def load(src, dst):
        copy = pltpu.make_async_copy(src, dst, lsem.at[len(loads)])
        copy.start()
        loads.append(copy)
        return copy

    first_loads = [load(wei_hbm, wei), load(scal_hbm, scal)]
    first_loads += [load(jac_hbm.at[:, 3 * r], jac.at[:, 3 * r]) for r in range(3)]
    first_loads += [load(side_hbm, side)]
    ids_load = load(ids_hbm, ids)
    late_loads = [load(jac_hbm.at[:, e], jac.at[:, e]) for e in (1, 2, 4, 5, 7, 8)]

    k_row = lax.broadcasted_iota(jnp.int32, (gx, 128), 0)
    k_lane = lax.broadcasted_iota(jnp.int32, (gx, 128), 1) % across
    own = (k_row // AX == k_lane).astype(F32)
    oth = (other_box(k_row, AX) == k_lane).astype(F32)
    sx[0:gx, :] = own.astype(BF16)
    sx[gx:, :] = (oth - own).astype(BF16)
    m_row = lax.broadcasted_iota(jnp.int32, (128, 4 * gy), 0)
    m_col = lax.broadcasted_iota(jnp.int32, (128, 4 * gy), 1)
    box_row = 2 * ((m_row % 32) // 8) - 1 + m_row // 32
    grid_row = m_col % gy
    own = (grid_row // AY == box_row).astype(F32)
    oth = (other_box(grid_row, AY) == box_row).astype(F32)
    sy[...] = jnp.where((m_col // gy) % 2 == 0, own, oth - own).astype(BF16)

    zero = jnp.zeros((gy, gx), F32)

    @pl.when(jnp.logical_not(has_low))
    def _():
        for buf in (f1, f2, cf, lf, t3, pf):
            buf[0] = zero
        c1[1] = zero
        for c in range(3):
            dr[0, c] = zero

    @pl.when(jnp.logical_not(has_high))
    def _():
        for buf in (f1, f2, cf, lf, t3, pf):
            buf[lz + 1] = zero
        c1[0] = zero
        for c in range(3):
            dr[lz + 1, c] = zero

    def up_copy(e, src, dst):
        return pltpu.make_async_remote_copy(
            src_ref=src, dst_ref=dst, send_sem=hs.at[e, 0], recv_sem=hr.at[e, 0],
            device_id={"cells": high_id}, device_id_type=pl.DeviceIdType.MESH,
        )

    def down_copy(e, src, dst):
        return pltpu.make_async_remote_copy(
            src_ref=src, dst_ref=dst, send_sem=hs.at[e, 1], recv_sem=hr.at[e, 1],
            device_id={"cells": low_id}, device_id_type=pl.DeviceIdType.MESH,
        )

    pairs = []

    def exchange(up_src, up_dst, down_src, down_dst):
        e = len(pairs)
        up = up_copy(e, up_src, up_dst)
        down = down_copy(e, down_src, down_dst)
        pairs.append((up, down))

        @pl.when(has_high)
        def _():
            up.start()

        @pl.when(has_low)
        def _():
            down.start()

        def arrive():
            @pl.when(has_low)
            def _():
                up.wait_recv()

            @pl.when(has_high)
            def _():
                down.wait_recv()

        return arrive

    def halo(buf):
        return exchange(buf.at[lz], buf.at[0], buf.at[1], buf.at[lz + 1])

    groups = []

    def spread(e, src, slots):
        src_ref = src

        def copy(step):
            return pltpu.make_async_remote_copy(
                src_ref=src_ref, dst_ref=slots.at[me], send_sem=gs.at[e],
                recv_sem=gr.at[e], device_id={"cells": lax.rem(me + step, n)},
                device_id_type=pl.DeviceIdType.MESH,
            )

        @pl.loop(1, n)
        def _(step):
            copy(step).start()

        slots[me] = src[...]

        def arrive():
            pltpu.make_async_copy(
                slots.at[pl.ds(0, n - 1)], slots.at[pl.ds(0, n - 1)], gr.at[e]
            ).wait()

        def sent():
            pltpu.make_async_copy(
                slots.at[pl.ds(0, n - 1)], slots.at[pl.ds(0, n - 1)], gs.at[e]
            ).wait()

        groups.append(sent)
        return arrive

    y_at = lax.broadcasted_iota(jnp.int32, (gy, gx), 0)
    x_at = lax.broadcasted_iota(jnp.int32, (gy, gx), 1)
    in_grid = [y_at > 0, y_at < gy - 1, x_at > 0, x_at < gx - 1]

    def shifted(v, way):
        if way == 0:
            return pltpu.roll(v, 1, 0)
        if way == 1:
            return pltpu.roll(v, gy - 1, 0)
        if way == 2:
            return pltpu.roll(v, 1, 1)
        return pltpu.roll(v, gx - 1, 1)

    for copy in first_loads:
        copy.wait()

    def pressure_layer(z):
        ws = [wei[r, z] * scal[r, z] for r in range(3)]
        low_keep = jnp.where(jnp.logical_and(z == 0, me == 0), 0.0, 1.0)
        high_keep = jnp.where(jnp.logical_and(z == top, me == n - 1), 0.0, 1.0)
        for k in range(7):
            s = ws[0] * jac[k, 0, z].astype(F32)
            for r in range(1, 3):
                s = s + ws[r] * jac[k, 3 * r, z].astype(F32)
            if k == 1:
                s = s * low_keep
            if k == 2:
                s = s * high_keep
            if k >= 3:
                s = jnp.where(in_grid[k - 3], s, 0.0)
            pc[k, z] = s
            if k == 0:
                w = DAMPING / s
        rs = LIFT * (wei[0, z] * side[0, z] + wei[1, z] * side[1, z] + wei[2, z] * side[2, z])
        rest[z] = rs
        wd[z] = w
        f1[z + 1] = rs * w

    @pl.loop(0, 2)
    def _(i):
        pressure_layer(i * top)

    pl.semaphore_wait(barrier, n - 1)
    f1_in = halo(f1)

    @pl.loop(1, top)
    def _(z):
        pressure_layer(z)

    c_in = exchange(pc.at[2, top], c1.at[1], pc.at[1, 0], c1.at[0])

    def inner(buf, z):
        v = buf[z + 1]
        s = pc[0, z] * v
        for way in range(4):
            s = s + pc[3 + way, z] * shifted(v, way)
        if z > 0:
            s = s + pc[1, z] * buf[z]
        if z < top:
            s = s + pc[2, z] * buf[z + 2]
        return s

    for z in range(lz):
        f2[z + 1] = f1[z + 1] + wd[z] * (rest[z] - inner(f1, z))
    f1_in()
    f2[1] = f2[1] - wd[0] * (pc[1, 0] * f1[0])
    f2[lz] = f2[lz] - wd[top] * (pc[2, top] * f1[lz + 1])
    f2_in = halo(f2)

    row_sum = []
    main = zero
    for z in range(lz):
        s = pc[0, z] + pc[3, z] + pc[4, z] + pc[5, z] + pc[6, z]
        if z > 0:
            s = s + pc[1, z]
        if z < top:
            s = s + pc[2, z]
        row_sum.append(s)
        main = main + s
        zed[0, z] = s

    def total(v):
        s = jnp.sum(v, axis=0, keepdims=True)
        return jnp.sum(s, axis=1, keepdims=True)

    g0s[0:1, :] = jnp.broadcast_to(total(main), (1, 128))
    g0s[1:2, :] = jnp.broadcast_to(total(pc[1, 0]), (1, 128))
    g0s[2:3, :] = jnp.broadcast_to(total(pc[2, top]), (1, 128))
    g0s[3:8, :] = jnp.zeros((5, 128), F32)
    g0_in = spread(0, g0s, g0)

    ids_load.wait()
    for z in range(lz):
        a = ids[z]
        ro = (a // across != y_at // AY).astype(F32)
        co = (a % across != x_at // AX).astype(F32)
        mask[0, z] = ro
        mask[1, z] = co
        mask[2, z] = ro * co
        gidx[z] = jnp.clip(a - (2 * (y_at // 8) - 1) * across, 0, 127)

    def gathered(layers):
        t = zero
        sums = [zero, zero, zero]
        for z, v in layers:
            t = t + v
            for i in range(3):
                sums[i] = sums[i] + mask[i, z] * v
        return [t] + sums

    group_at = lax.broadcasted_iota(jnp.int32, (gy, 128), 1) // across

    def restrict(parts):
        t, ro, co, rc = parts
        stacked = jnp.concatenate(
            [jnp.concatenate([t, co], axis=1), jnp.concatenate([ro, rc], axis=1)], axis=0
        )
        out = jnp.dot(split_rows(stacked), sx[...], preferred_element_type=F32)
        out = out[: 2 * gy] + out[2 * gy :]
        out = jnp.dot(sy[...], split_rows(out), preferred_element_type=F32)
        res = out[0:gy]
        for g in range(1, 4):
            res = jnp.where(group_at == g, out[g * gy : (g + 1) * gy], res)
        return res

    def prolong(table, buf, z):
        for h in range(2):
            buf[z + 1, :, h * half : (h + 1) * half] = jnp.take_along_axis(
                table, gidx[z, :, h * half : (h + 1) * half], axis=1
            )

    def diag_layer(z):
        a = ids[z]
        s = pc[0, z]
        for way in range(4):
            s = s + jnp.where(shifted(a, way) == a, pc[3 + way, z], 0.0)
        if z > 0:
            s = s + jnp.where(ids[z - 1] == a, pc[1, z], 0.0)
        if z < top:
            s = s + jnp.where(ids[z + 1] == a, pc[2, z], 0.0)
        return s

    wdiag = DAMPING / restrict(gathered([(z, diag_layer(z)) for z in range(lz)]))

    for z in range(lz):
        zed[1, z] = rest[z] - inner(f2, z)

    f2_in()
    zed[1, 0] = zed[1, 0] - pc[1, 0] * f2[0]
    zed[1, top] = zed[1, top] - pc[2, top] * f2[lz + 1]
    rhs = restrict(gathered([(z, zed[1, z]) for z in range(lz)]))
    coarse_first = wdiag * rhs
    prolong(coarse_first, cf, 0)
    prolong(coarse_first, cf, top)
    cf_in = halo(cf)
    for z in range(1, top):
        prolong(coarse_first, cf, z)
    own_sum = zero
    for z in range(lz):
        q = zed[1, z] - inner(cf, z)
        zed[1, z] = q
        own_sum = own_sum + q
    c_in()
    lane = lax.broadcasted_iota(jnp.int32, (1, 128), 1)
    tile = jnp.where(lane == me, total(own_sum), 0.0)
    tile = tile - jnp.where(lane == me + 1, total(c1[0] * cf[lz]), 0.0)
    tile = tile - jnp.where(lane == me - 1, total(c1[1] * cf[1]), 0.0)
    g4s[...] = jnp.broadcast_to(tile, (8, 128))
    g4_in = spread(1, g4s, g4)

    g0_in()
    inv[0] = jnp.zeros((1, 128), F32)
    inv[n + 1] = jnp.zeros((1, 128), F32)
    previous_c = jnp.zeros((1, 128), F32)
    previous_d = jnp.zeros((1, 128), F32)
    for j in range(n):
        m, l, u = g0[j, 0:1, :], g0[j, 1:2, :], g0[j, 2:3, :]
        scale = 1.0 / (m - l * previous_c)
        previous_c = u * scale
        previous_d = (jnp.where(lane == j, 1.0, 0.0) - l * previous_d) * scale
        shv[j] = previous_c
        inv[j + 1] = previous_d
    for j in range(n - 2, -1, -1):
        inv[j + 1] = inv[j + 1] - shv[j] * inv[j + 2]

    row_part = restrict(gathered([(z, zed[0, z]) for z in range(lz)]))
    low_part = restrict(gathered([(0, pc[1, 0])]))
    high_part = restrict(gathered([(top, pc[2, top])]))

    cf_in()
    zed[1, 0] = zed[1, 0] - pc[1, 0] * cf[0]
    zed[1, top] = zed[1, top] - pc[2, top] * cf[lz + 1]
    rhs = restrict(gathered([(z, zed[1, z]) for z in range(lz)]))

    g4_in()
    res = g4[0, 0:1, :]
    for j in range(1, n):
        res = res + g4[j, 0:1, :]

    def fix_of(row):
        return jnp.sum(inv[row] * res, axis=1, keepdims=True)

    fix_low, fix_own, fix_high = fix_of(me), fix_of(me + 1), fix_of(me + 2)
    coarse_third = (
        coarse_first
        + fix_own
        + wdiag * (rhs - fix_own * row_part - fix_low * low_part - fix_high * high_part)
    )
    prolong(coarse_third, lf, 0)
    prolong(coarse_third, lf, top)
    lf_in = halo(lf)
    for z in range(1, top):
        prolong(coarse_third, lf, z)
    for z in range(lz):
        t3[z + 1] = f2[z + 1] + lf[z + 1] - wd[z] * inner(lf, z)
    lf_in()
    t3[1] = t3[1] - wd[0] * (pc[1, 0] * lf[0])
    t3[lz] = t3[lz] - wd[top] * (pc[2, top] * lf[lz + 1])
    t3_in = halo(t3)
    for z in range(lz):
        pf[z + 1] = t3[z + 1] + wd[z] * (rest[z] - inner(t3, z))

    for copy in late_loads:
        copy.wait()

    @pl.loop(0, lz)
    def _(z):
        mat = [jac[0, e, z].astype(F32) for e in range(9)]
        co_aa = mat[4] * mat[8] - mat[5] * mat[7]
        co_ab = mat[5] * mat[6] - mat[3] * mat[8]
        co_ac = mat[3] * mat[7] - mat[4] * mat[6]
        det = 1.0 / (mat[0] * co_aa + mat[1] * co_ab + mat[2] * co_ac)
        binv[0, z] = co_aa * det
        binv[3, z] = co_ab * det
        binv[6, z] = co_ac * det
        binv[1, z] = (mat[2] * mat[7] - mat[1] * mat[8]) * det
        binv[4, z] = (mat[0] * mat[8] - mat[2] * mat[6]) * det
        binv[7, z] = (mat[1] * mat[6] - mat[0] * mat[7]) * det
        binv[2, z] = (mat[1] * mat[5] - mat[2] * mat[4]) * det
        binv[5, z] = (mat[2] * mat[3] - mat[0] * mat[5]) * det
        binv[8, z] = (mat[0] * mat[4] - mat[1] * mat[3]) * det

    t3_in()
    pf[1] = pf[1] - wd[0] * (pc[1, 0] * t3[0])
    pf[lz] = pf[lz] - wd[top] * (pc[2, top] * t3[lz + 1])
    pf_in = halo(pf)

    def near_terms(v, way):
        return jnp.where(in_grid[way], shifted(v, way), 0.0)

    for z in range(lz):
        v = pf[z + 1]
        acc = [LIFT * side[r, z] / scal[r, z] for r in range(3)]
        for way in range(4):
            s = near_terms(v, way)
            for r in range(3):
                acc[r] = acc[r] - jac[3 + way, 3 * r, z].astype(F32) * s
        if z > 0:
            for r in range(3):
                acc[r] = acc[r] - jac[1, 3 * r, z].astype(F32) * pf[z]
        if z < top:
            for r in range(3):
                acc[r] = acc[r] - jac[2, 3 * r, z].astype(F32) * pf[z + 2]
        for r in range(3):
            zed[r, z] = acc[r]

    def solve_layer(z):
        v = [zed[r, z] for r in range(3)]
        for c in range(3):
            d = binv[3 * c, z] * v[0] + binv[3 * c + 1, z] * v[1] + binv[3 * c + 2, z] * v[2]
            dr[z + 1, c] = d
            dout[c, z] = d

    pf_in()
    for r in range(3):
        zed[r, 0] = zed[r, 0] - jac[1, 3 * r, 0].astype(F32) * pf[0]
        zed[r, top] = zed[r, top] - jac[2, 3 * r, top].astype(F32) * pf[lz + 1]
    solve_layer(0)
    solve_layer(top)
    dr_in = halo(dr)

    @pl.loop(1, top)
    def _(z):
        solve_layer(z)

    dir_out = pltpu.make_async_copy(dout, dir_hbm, osem.at[0])
    dir_out.start()

    for z in range(lz):
        acc = [zed[r, z] for r in range(3)]
        for c in range(3):
            v = dr[z + 1, c]
            for way in range(4):
                s = near_terms(v, way)
                for r in range(3):
                    acc[r] = acc[r] + jac[3 + way, 3 * r + c, z].astype(F32) * s
            if z > 0:
                for r in range(3):
                    acc[r] = acc[r] + jac[1, 3 * r + c, z].astype(F32) * dr[z, c]
            if z < top:
                for r in range(3):
                    acc[r] = acc[r] + jac[2, 3 * r + c, z].astype(F32) * dr[z + 2, c]
        for r in range(3):
            zed[r, z] = acc[r]

    dr_in()
    for c in range(3):
        for r in range(3):
            zed[r, 0] = zed[r, 0] + jac[1, 3 * r + c, 0].astype(F32) * dr[0, c]
            zed[r, top] = zed[r, top] + jac[2, 3 * r + c, top].astype(F32) * dr[lz + 1, c]
    s1, s2, s3 = zero, zero, zero
    for z in range(lz):
        for r in range(3):
            b = side[r, z]
            v = scal[r, z] * zed[r, z]
            iout[r, z] = v
            s1 = s1 + b * b
            s2 = s2 + v * (LIFT * b)
            s3 = s3 + v * v
    img_out = pltpu.make_async_copy(iout, img_hbm, osem.at[1])
    img_out.start()

    def lanes(v):
        s = v[:, :half] + v[:, half:]
        return jnp.sum(s, axis=0, keepdims=True)

    g9s[0:1, :] = lanes(s1)
    g9s[1:2, :] = lanes(s2)
    g9s[2:3, :] = lanes(s3)
    g9s[3:8, :] = jnp.zeros((5, 128), F32)
    g9_in = spread(2, g9s, g9)
    g9_in()
    tot = g9[0]
    for j in range(1, n):
        tot = tot + g9[j]
    tot_ref[...] = tot

    for up, down in pairs:
        @pl.when(has_high)
        def _(up=up):
            up.wait_send()

        @pl.when(has_low)
        def _(down=down):
            down.wait_send()

    for sent in groups:
        sent()
    dir_out.wait()
    img_out.wait()


def shards(n, jacobian, right_side, scales, weights, aggregate_of):
    lz, gy, gx = aggregate_of.shape
    field = (lz, gy, gx)
    border = (lz + 2, gy, gx)
    vm = lambda shape, dtype=F32: pltpu.VMEM(shape, dtype)
    any_spec = pl.BlockSpec(memory_space=pl.ANY)
    direction, image, totals = pl.pallas_call(
        functools.partial(kernel, n, lz, gy, gx),
        out_shape=(
            jax.ShapeDtypeStruct((3,) + field, F32),
            jax.ShapeDtypeStruct((3,) + field, F32),
            jax.ShapeDtypeStruct((8, 128), F32),
        ),
        in_specs=[any_spec] * 5,
        out_specs=(any_spec, any_spec, pl.BlockSpec(memory_space=pltpu.VMEM)),
        scratch_shapes=[
            vm((7, 9) + field, BF16), vm((3,) + field), vm((3,) + field), vm((3,) + field),
            vm(field, jnp.int32),
            vm((7,) + field), vm(field), vm(field), vm((9,) + field), vm((3,) + field),
            vm((3,) + field), vm((3,) + field),
            vm(border), vm(border), vm(border), vm(border), vm(border), vm(border),
            vm((lz + 2, 3, gy, gx)), vm((2, gy, gx)), vm((8, 128)),
            vm((3,) + field), vm(field, jnp.int32), vm((2 * gx, 128), BF16),
            vm((128, 4 * gy), BF16), vm((n + 2, 1, 128)), vm((n, 1, 128)),
            vm((n, 8, 128)), vm((n, 8, 128)), vm((n, 8, 128)),
            vm((8, 128)), vm((8, 128)), vm((8, 128)),
            pltpu.SemaphoreType.DMA((16,)), pltpu.SemaphoreType.DMA((2,)),
            pltpu.SemaphoreType.DMA((8, 2)), pltpu.SemaphoreType.DMA((8, 2)),
            pltpu.SemaphoreType.DMA((3,)), pltpu.SemaphoreType.DMA((3,)),
        ],
        compiler_params=pltpu.CompilerParams(
            collective_id=0, has_side_effects=True, vmem_limit_bytes=48 * 1024 * 1024
        ),
    )(jacobian, right_side, scales, weights, aggregate_of)
    s1, s2, s3 = (jnp.sum(totals[i]) for i in range(3))
    norm = s1 + 1e-6
    along = s2 / (LIFT * norm)
    step = s2 / (LIFT * (s3 - 1e-6 * along * along))
    return (step * direction, right_side - step * image)


def solution(mesh):
    return jax.shard_map(
        functools.partial(shards, mesh.shape["cells"]),
        mesh=mesh,
        in_specs=(
            P(None, None, ("groups", "cells"), None, None),
            P(None, ("groups", "cells"), None, None),
            P(None, ("groups", "cells"), None, None),
            P(None, ("groups", "cells"), None, None),
            P(("groups", "cells"), None, None),
        ),
        out_specs=(
            P(None, ("groups", "cells"), None, None),
            P(None, ("groups", "cells"), None, None),
        ),
        check_vma=False,
    )
```

```python
import functools

import jax
import jax.numpy as jnp
from jax import lax
from jax.experimental import pallas as pl
from jax.experimental.pallas import tpu as pltpu
from jax.sharding import PartitionSpec as P

AY = 4
AX = 8
DAMPING = 2.0 / 3.0
LIFT = 1024.0
F32 = jnp.float32
BF16 = jnp.bfloat16


def split_rows(x):
    hi = x.astype(BF16)
    lo = (x - hi.astype(F32)).astype(BF16)
    return jnp.concatenate([hi, lo], axis=0)


def other_box(place, width):
    part = place % width
    own = place // width
    return jnp.where(part == 0, own - 1, jnp.where(part == width - 1, own + 1, -9))


def kernel(
    n, lz, gy, gx,
    jac_hbm, side_hbm, scal_hbm, wei_hbm, ids_hbm,
    dout, iout, step_ref,
    jac, side, scal, wei, ids,
    pc, wd, rest, binv, zed,
    f1, f2, cf, lf, t3, pf, dr, c1, mh, mo, f2s, t3s, drs, mm, mmh, zz,
    mask, gidx, sx, sy, inv, shv,
    g0, g4, g9, g0s, g4s, g9s,
    lsem, hs, hr, gs, gr,
):
    me = lax.axis_index("cells")
    has_low = me > 0
    has_high = me < n - 1
    low_id = jnp.maximum(me - 1, 0)
    high_id = jnp.minimum(me + 1, n - 1)
    top = lz - 1
    across = gx // AX
    half = gx // 2
    tiles = gy // 8

    barrier = pltpu.get_barrier_semaphore()

    @pl.loop(1, n)
    def _(step):
        pl.semaphore_signal(
            barrier, inc=1, device_id={"cells": lax.rem(me + step, n)},
            device_id_type=pl.DeviceIdType.MESH,
        )

    loads = []

    def load(src, dst):
        copy = pltpu.make_async_copy(src, dst, lsem.at[len(loads)])
        copy.start()
        loads.append(copy)
        return copy

    first_loads = [load(wei_hbm, wei), load(scal_hbm, scal)]
    first_loads += [load(jac_hbm.at[:, 3 * r], jac.at[:, 3 * r]) for r in range(3)]
    first_loads += [load(side_hbm, side)]
    ids_load = load(ids_hbm, ids)
    late_loads = [load(jac_hbm.at[:, e], jac.at[:, e]) for e in (1, 2, 4, 5, 7, 8)]

    k_row = lax.broadcasted_iota(jnp.int32, (gx, 128), 0)
    k_lane = lax.broadcasted_iota(jnp.int32, (gx, 128), 1) % across
    own = (k_row // AX == k_lane).astype(F32)
    oth = (other_box(k_row, AX) == k_lane).astype(F32)
    sx[0:gx, :] = own.astype(BF16)
    sx[gx:, :] = (oth - own).astype(BF16)
    m_row = lax.broadcasted_iota(jnp.int32, (128, 4 * gy), 0)
    m_col = lax.broadcasted_iota(jnp.int32, (128, 4 * gy), 1)
    box_row = 2 * ((m_row % 32) // 8) - 1 + m_row // 32
    grid_row = m_col % gy
    own = (grid_row // AY == box_row).astype(F32)
    oth = (other_box(grid_row, AY) == box_row).astype(F32)
    sy[...] = jnp.where((m_col // gy) % 2 == 0, own, oth - own).astype(BF16)

    zero = jnp.zeros((gy, gx), F32)

    @pl.when(jnp.logical_not(has_low))
    def _():
        for buf in (f1, f2, cf, lf, t3, pf):
            buf[0] = zero
        c1[1] = zero
        mh[1] = zero
        for c in range(3):
            dr[0, c] = zero
            mmh[1, c] = zero

    @pl.when(jnp.logical_not(has_high))
    def _():
        for buf in (f1, f2, cf, lf, t3, pf):
            buf[lz + 1] = zero
        c1[0] = zero
        mh[0] = zero
        for c in range(3):
            dr[lz + 1, c] = zero
            mmh[0, c] = zero

    def up_copy(e, src, dst):
        return pltpu.make_async_remote_copy(
            src_ref=src, dst_ref=dst, send_sem=hs.at[e, 0], recv_sem=hr.at[e, 0],
            device_id={"cells": high_id}, device_id_type=pl.DeviceIdType.MESH,
        )

    def down_copy(e, src, dst):
        return pltpu.make_async_remote_copy(
            src_ref=src, dst_ref=dst, send_sem=hs.at[e, 1], recv_sem=hr.at[e, 1],
            device_id={"cells": low_id}, device_id_type=pl.DeviceIdType.MESH,
        )

    pairs = []

    def exchange(up_src, up_dst, down_src, down_dst):
        e = len(pairs)
        up = up_copy(e, up_src, up_dst)
        down = down_copy(e, down_src, down_dst)
        pairs.append((up, down))

        @pl.when(has_high)
        def _():
            up.start()

        @pl.when(has_low)
        def _():
            down.start()

        def arrive():
            @pl.when(has_low)
            def _():
                up.wait_recv()

            @pl.when(has_high)
            def _():
                down.wait_recv()

        return arrive

    def halo(buf):
        return exchange(buf.at[lz], buf.at[0], buf.at[1], buf.at[lz + 1])

    groups = []

    def spread(e, src, slots):
        src_ref = src

        def copy(step):
            return pltpu.make_async_remote_copy(
                src_ref=src_ref, dst_ref=slots.at[me], send_sem=gs.at[e],
                recv_sem=gr.at[e], device_id={"cells": lax.rem(me + step, n)},
                device_id_type=pl.DeviceIdType.MESH,
            )

        @pl.loop(1, n)
        def _(step):
            copy(step).start()

        slots[me] = src[...]

        def arrive():
            pltpu.make_async_copy(
                slots.at[pl.ds(0, n - 1)], slots.at[pl.ds(0, n - 1)], gr.at[e]
            ).wait()

        def sent():
            pltpu.make_async_copy(
                slots.at[pl.ds(0, n - 1)], slots.at[pl.ds(0, n - 1)], gs.at[e]
            ).wait()

        groups.append(sent)
        return arrive

    y_at = lax.broadcasted_iota(jnp.int32, (gy, gx), 0)
    x_at = lax.broadcasted_iota(jnp.int32, (gy, gx), 1)
    in_grid = [y_at > 0, y_at < gy - 1, x_at > 0, x_at < gx - 1]

    def shifted(v, way):
        if way == 0:
            return pltpu.roll(v, 1, 0)
        if way == 1:
            return pltpu.roll(v, gy - 1, 0)
        if way == 2:
            return pltpu.roll(v, 1, 1)
        return pltpu.roll(v, gx - 1, 1)

    for copy in first_loads:
        copy.wait()

    def pressure_layer(z):
        ws = [wei[r, z] * scal[r, z] for r in range(3)]
        low_keep = jnp.where(jnp.logical_and(z == 0, me == 0), 0.0, 1.0)
        high_keep = jnp.where(jnp.logical_and(z == top, me == n - 1), 0.0, 1.0)
        for k in range(7):
            s = ws[0] * jac[k, 0, z].astype(F32)
            for r in range(1, 3):
                s = s + ws[r] * jac[k, 3 * r, z].astype(F32)
            if k == 1:
                s = s * low_keep
            if k == 2:
                s = s * high_keep
            if k >= 3:
                s = jnp.where(in_grid[k - 3], s, 0.0)
            pc[k, z] = s
            if k == 0:
                w = DAMPING / s
        rs = LIFT * (wei[0, z] * side[0, z] + wei[1, z] * side[1, z] + wei[2, z] * side[2, z])
        rest[z] = rs
        wd[z] = w
        f1[z + 1] = rs * w

    @pl.loop(0, 2)
    def _(i):
        pressure_layer(i * top)

    pl.semaphore_wait(barrier, n - 1)
    f1_in = halo(f1)

    @pl.loop(1, top)
    def _(z):
        pressure_layer(z)

    mo[0] = wd[0] * pc[1, 0]
    mo[1] = wd[top] * pc[2, top]
    m_in = exchange(mo.at[1], mh.at[1], mo.at[0], mh.at[0])

    def complete(below, buf):
        buf[1] = buf[1] - mo[0] * below[0]
        buf[lz] = buf[lz] - mo[1] * below[lz + 1]
        buf[0] = buf[0] - mh[1] * below[1]
        buf[lz + 1] = buf[lz + 1] - mh[0] * below[lz]

    def inner(buf, z):
        v = buf[z + 1]
        s = pc[0, z] * v
        for way in range(4):
            s = s + pc[3 + way, z] * shifted(v, way)
        if z > 0:
            s = s + pc[1, z] * buf[z]
        if z < top:
            s = s + pc[2, z] * buf[z + 2]
        return s

    for z in (0, top):
        f2[z + 1] = f1[z + 1] + wd[z] * (rest[z] - inner(f1, z))
    f2s[0] = f2[1]
    f2s[1] = f2[lz]
    f2_in = exchange(f2s.at[1], f2.at[0], f2s.at[0], f2.at[lz + 1])
    for z in range(1, top):
        f2[z + 1] = f1[z + 1] + wd[z] * (rest[z] - inner(f1, z))

    row_sum = []
    main = zero
    for z in range(lz):
        s = pc[0, z] + pc[3, z] + pc[4, z] + pc[5, z] + pc[6, z]
        if z > 0:
            s = s + pc[1, z]
        if z < top:
            s = s + pc[2, z]
        row_sum.append(s)
        main = main + s
        zed[0, z] = s

    def total(v):
        s = jnp.sum(v, axis=0, keepdims=True)
        return jnp.sum(s, axis=1, keepdims=True)

    g0s[0:1, :] = jnp.broadcast_to(total(main), (1, 128))
    g0s[1:2, :] = jnp.broadcast_to(total(pc[1, 0]), (1, 128))
    g0s[2:3, :] = jnp.broadcast_to(total(pc[2, top]), (1, 128))
    g0s[3:8, :] = jnp.zeros((5, 128), F32)
    g0_in = spread(0, g0s, g0)
    c_in = exchange(pc.at[2, top], c1.at[1], pc.at[1, 0], c1.at[0])

    ids_load.wait()
    for z in range(lz):
        a = ids[z]
        ro = (a // across != y_at // AY).astype(F32)
        co = (a % across != x_at // AX).astype(F32)
        mask[0, z] = ro
        mask[1, z] = co
        mask[2, z] = ro * co
        gidx[z] = jnp.clip(a - (2 * (y_at // 8) - 1) * across, 0, 127)

    def gathered(layers):
        t = zero
        sums = [zero, zero, zero]
        for z, v in layers:
            t = t + v
            for i in range(3):
                sums[i] = sums[i] + mask[i, z] * v
        return [t] + sums

    group_at = lax.broadcasted_iota(jnp.int32, (gy, 128), 1) // across

    def restrict(parts):
        t, ro, co, rc = parts
        stacked = jnp.concatenate(
            [jnp.concatenate([t, co], axis=1), jnp.concatenate([ro, rc], axis=1)], axis=0
        )
        out = jnp.dot(split_rows(stacked), sx[...], preferred_element_type=F32)
        out = out[: 2 * gy] + out[2 * gy :]
        out = jnp.dot(sy[...], split_rows(out), preferred_element_type=F32)
        res = out[0:gy]
        for g in range(1, 4):
            res = jnp.where(group_at == g, out[g * gy : (g + 1) * gy], res)
        return res

    def prolong(table, buf, z):
        for h in range(2):
            buf[z + 1, :, h * half : (h + 1) * half] = jnp.take_along_axis(
                table, gidx[z, :, h * half : (h + 1) * half], axis=1
            )

    def diag_layer(z):
        a = ids[z]
        s = pc[0, z]
        for way in range(4):
            s = s + jnp.where(shifted(a, way) == a, pc[3 + way, z], 0.0)
        if z > 0:
            s = s + jnp.where(ids[z - 1] == a, pc[1, z], 0.0)
        if z < top:
            s = s + jnp.where(ids[z + 1] == a, pc[2, z], 0.0)
        return s

    wdiag = DAMPING / restrict(gathered([(z, diag_layer(z)) for z in range(lz)]))

    for z in range(lz):
        for r in range(3):
            zz[r, z] = LIFT * side[r, z] / scal[r, z]

    f1_in()
    m_in()
    f2_in()
    complete(f1, f2)
    for z in range(lz):
        zed[1, z] = rest[z] - inner(f2, z)
    zed[1, 0] = zed[1, 0] - pc[1, 0] * f2[0]
    zed[1, top] = zed[1, top] - pc[2, top] * f2[lz + 1]
    rhs = restrict(gathered([(z, zed[1, z]) for z in range(lz)]))
    coarse_first = wdiag * rhs
    prolong(coarse_first, cf, 0)
    prolong(coarse_first, cf, top)
    cf_in = halo(cf)
    for z in range(1, top):
        prolong(coarse_first, cf, z)
    own_sum = zero
    for z in range(lz):
        q = zed[1, z] - inner(cf, z)
        zed[1, z] = q
        own_sum = own_sum + q
    c_in()
    lane = lax.broadcasted_iota(jnp.int32, (1, 128), 1)
    tile = jnp.where(lane == me, total(own_sum), 0.0)
    tile = tile - jnp.where(lane == me + 1, total(c1[0] * cf[lz]), 0.0)
    tile = tile - jnp.where(lane == me - 1, total(c1[1] * cf[1]), 0.0)
    g4s[...] = jnp.broadcast_to(tile, (8, 128))
    g4_in = spread(1, g4s, g4)

    g0_in()
    inv[0] = jnp.zeros((1, 128), F32)
    inv[n + 1] = jnp.zeros((1, 128), F32)
    previous_c = jnp.zeros((1, 128), F32)
    previous_d = jnp.zeros((1, 128), F32)
    for j in range(n):
        m, l, u = g0[j, 0:1, :], g0[j, 1:2, :], g0[j, 2:3, :]
        scale = 1.0 / (m - l * previous_c)
        previous_c = u * scale
        previous_d = (jnp.where(lane == j, 1.0, 0.0) - l * previous_d) * scale
        shv[j] = previous_c
        inv[j + 1] = previous_d
    for j in range(n - 2, -1, -1):
        inv[j + 1] = inv[j + 1] - shv[j] * inv[j + 2]

    row_part = restrict(gathered([(z, zed[0, z]) for z in range(lz)]))
    low_part = restrict(gathered([(0, pc[1, 0])]))
    high_part = restrict(gathered([(top, pc[2, top])]))

    cf_in()
    zed[1, 0] = zed[1, 0] - pc[1, 0] * cf[0]
    zed[1, top] = zed[1, top] - pc[2, top] * cf[lz + 1]
    rhs = restrict(gathered([(z, zed[1, z]) for z in range(lz)]))

    for copy in late_loads:
        copy.wait()

    @pl.loop(0, lz)
    def _(z):
        mat = [jac[0, e, z].astype(F32) for e in range(9)]
        co_aa = mat[4] * mat[8] - mat[5] * mat[7]
        co_ab = mat[5] * mat[6] - mat[3] * mat[8]
        co_ac = mat[3] * mat[7] - mat[4] * mat[6]
        det = 1.0 / (mat[0] * co_aa + mat[1] * co_ab + mat[2] * co_ac)
        binv[0, z] = co_aa * det
        binv[3, z] = co_ab * det
        binv[6, z] = co_ac * det
        binv[1, z] = (mat[2] * mat[7] - mat[1] * mat[8]) * det
        binv[4, z] = (mat[0] * mat[8] - mat[2] * mat[6]) * det
        binv[7, z] = (mat[1] * mat[6] - mat[0] * mat[7]) * det
        binv[2, z] = (mat[1] * mat[5] - mat[2] * mat[4]) * det
        binv[5, z] = (mat[2] * mat[3] - mat[0] * mat[5]) * det
        binv[8, z] = (mat[0] * mat[4] - mat[1] * mat[3]) * det

    for side_at, z, k in ((0, 0, 1), (1, top, 2)):
        for c in range(3):
            v = binv[3 * c, z] * jac[k, 0, z].astype(F32)
            for r in range(1, 3):
                v = v + binv[3 * c + r, z] * jac[k, 3 * r, z].astype(F32)
            mm[side_at, c] = v
    mm_in = exchange(mm.at[1], mmh.at[1], mm.at[0], mmh.at[0])

    g4_in()
    res = g4[0, 0:1, :]
    for j in range(1, n):
        res = res + g4[j, 0:1, :]

    def fix_of(row):
        return jnp.sum(inv[row] * res, axis=1, keepdims=True)

    fix_low, fix_own, fix_high = fix_of(me), fix_of(me + 1), fix_of(me + 2)
    coarse_third = (
        coarse_first
        + fix_own
        + wdiag * (rhs - fix_own * row_part - fix_low * low_part - fix_high * high_part)
    )
    prolong(coarse_third, lf, 0)
    prolong(coarse_third, lf, top)
    lf_in = halo(lf)
    for z in range(1, top):
        prolong(coarse_third, lf, z)
    for z in (0, top):
        t3[z + 1] = f2[z + 1] + lf[z + 1] - wd[z] * inner(lf, z)
    t3s[0] = t3[1]
    t3s[1] = t3[lz]
    t3_in = exchange(t3s.at[1], t3.at[0], t3s.at[0], t3.at[lz + 1])
    for z in range(1, top):
        t3[z + 1] = f2[z + 1] + lf[z + 1] - wd[z] * inner(lf, z)
    lf_in()
    t3_in()
    complete(lf, t3)
    for z in range(lz):
        pf[z + 1] = t3[z + 1] + wd[z] * (rest[z] - inner(t3, z))
    pf[1] = pf[1] - mo[0] * t3[0]
    pf[lz] = pf[lz] - mo[1] * t3[lz + 1]
    pf_in = halo(pf)

    def near_terms(v, way):
        return jnp.where(in_grid[way], shifted(v, way), 0.0)

    def section_layer(z):
        v = pf[z + 1]
        acc = [zz[r, z] for r in range(3)]
        for way in range(4):
            s = near_terms(v, way)
            for r in range(3):
                acc[r] = acc[r] - jac[3 + way, 3 * r, z].astype(F32) * s
        if z > 0:
            for r in range(3):
                acc[r] = acc[r] - jac[1, 3 * r, z].astype(F32) * pf[z]
        if z < top:
            for r in range(3):
                acc[r] = acc[r] - jac[2, 3 * r, z].astype(F32) * pf[z + 2]
        for r in range(3):
            zed[r, z] = acc[r]

    def solve_layer(z):
        v = [zed[r, z] for r in range(3)]
        for c in range(3):
            d = binv[3 * c, z] * v[0] + binv[3 * c + 1, z] * v[1] + binv[3 * c + 2, z] * v[2]
            dr[z + 1, c] = d

    section_layer(0)
    section_layer(top)
    solve_layer(0)
    solve_layer(top)
    for c in range(3):
        drs[0, c] = dr[1, c]
        drs[1, c] = dr[lz, c]
    dr_in = exchange(drs.at[1], dr.at[0], drs.at[0], dr.at[lz + 1])
    for z in range(1, top):
        section_layer(z)
    for z in range(1, top):
        solve_layer(z)

    def in_layer(z, acc):
        for c in range(3):
            v = dr[z + 1, c]
            for way in range(4):
                s = near_terms(v, way)
                for r in range(3):
                    acc[r] = acc[r] + jac[3 + way, 3 * r + c, z].astype(F32) * s
        return acc

    def from_layer(z, k, acc):
        for c in range(3):
            v = dr[z + 2 * k - 2, c]
            for r in range(3):
                acc[r] = acc[r] + jac[k, 3 * r + c, z].astype(F32) * v
        return acc

    def early(z):
        acc = [zed[r, z] for r in range(3)]
        if 0 < z < top:
            acc = in_layer(z, acc)
        if z > 1:
            acc = from_layer(z, 1, acc)
        if z < top - 1:
            acc = from_layer(z, 2, acc)
        for r in range(3):
            zed[r, z] = acc[r]

    for z in range(lz):
        early(z)

    mm_in()
    pf_in()
    for r in range(3):
        zed[r, 0] = zed[r, 0] - jac[1, 3 * r, 0].astype(F32) * pf[0]
        zed[r, top] = zed[r, top] - jac[2, 3 * r, top].astype(F32) * pf[lz + 1]
    for c in range(3):
        dr[1, c] = dr[1, c] - mm[0, c] * pf[0]
        dr[lz, c] = dr[lz, c] - mm[1, c] * pf[lz + 1]
    def late(z):
        acc = [zed[r, z] for r in range(3)]
        if z == 0 or z == top:
            acc = in_layer(z, acc)
        if z == 1:
            acc = from_layer(z, 1, acc)
        if z == top - 1:
            acc = from_layer(z, 2, acc)
        for r in range(3):
            zed[r, z] = acc[r]

    for z in range(lz):
        late(z)
    dr_in()
    for c in range(3):
        low = dr[0, c] - mmh[1, c] * pf[1]
        high = dr[lz + 1, c] - mmh[0, c] * pf[lz]
        for r in range(3):
            zed[r, 0] = zed[r, 0] + jac[1, 3 * r + c, 0].astype(F32) * low
            zed[r, top] = zed[r, top] + jac[2, 3 * r + c, top].astype(F32) * high
    s1, s2, s3 = zero, zero, zero
    for z in range(lz):
        for r in range(3):
            b = side[r, z]
            v = scal[r, z] * zed[r, z]
            iout[r, z] = v
            s1 = s1 + b * b
            s2 = s2 + v * (LIFT * b)
            s3 = s3 + v * v

    def lanes(v):
        s = v[:, :half] + v[:, half:]
        return jnp.sum(s, axis=0, keepdims=True)

    g9s[0:1, :] = lanes(s1)
    g9s[1:2, :] = lanes(s2)
    g9s[2:3, :] = lanes(s3)
    g9s[3:8, :] = jnp.zeros((5, 128), F32)
    g9_in = spread(2, g9s, g9)
    for z in range(lz):
        for c in range(3):
            dout[c, z] = dr[z + 1, c]
    g9_in()
    tot = g9[0]
    for j in range(1, n):
        tot = tot + g9[j]
    tot = jnp.sum(tot, axis=1, keepdims=True)
    along = tot[1:2] / (LIFT * (tot[0:1] + 1e-6))
    step = tot[1:2] / (LIFT * (tot[2:3] - 1e-6 * along * along))
    step_ref[...] = jnp.broadcast_to(step, (gy, gx))

    for up, down in pairs:
        @pl.when(has_high)
        def _(up=up):
            up.wait_send()

        @pl.when(has_low)
        def _(down=down):
            down.wait_send()

    for sent in groups:
        sent()


def shards(n, jacobian, right_side, scales, weights, aggregate_of):
    lz, gy, gx = aggregate_of.shape
    field = (lz, gy, gx)
    border = (lz + 2, gy, gx)
    vm = lambda shape, dtype=F32: pltpu.VMEM(shape, dtype)
    vmem_spec = pl.BlockSpec(memory_space=pltpu.VMEM)
    direction, image, step = pl.pallas_call(
        functools.partial(kernel, n, lz, gy, gx),
        out_shape=(
            jax.ShapeDtypeStruct((3,) + field, F32),
            jax.ShapeDtypeStruct((3,) + field, F32),
            jax.ShapeDtypeStruct((gy, gx), F32),
        ),
        in_specs=[pl.BlockSpec(memory_space=pltpu.HBM)] * 5,
        out_specs=(vmem_spec,) * 3,
        scratch_shapes=[
            vm((7, 9) + field, BF16), vm((3,) + field), vm((3,) + field), vm((3,) + field),
            vm(field, jnp.int32),
            vm((7,) + field), vm(field), vm(field), vm((9,) + field), vm((3,) + field),
            vm(border), vm(border), vm(border), vm(border), vm(border), vm(border),
            vm((lz + 2, 3, gy, gx)), vm((2, gy, gx)), vm((2, gy, gx)), vm((2, gy, gx)),
            vm((2, gy, gx)), vm((2, gy, gx)), vm((2, 3, gy, gx)), vm((2, 3, gy, gx)),
            vm((2, 3, gy, gx)), vm((3,) + field),
            vm((3,) + field), vm(field, jnp.int32), vm((2 * gx, 128), BF16),
            vm((128, 4 * gy), BF16), vm((n + 2, 1, 128)), vm((n, 1, 128)),
            vm((n, 8, 128)), vm((n, 8, 128)), vm((n, 8, 128)),
            vm((8, 128)), vm((8, 128)), vm((8, 128)),
            pltpu.SemaphoreType.DMA((16,)),
            pltpu.SemaphoreType.DMA((12, 2)), pltpu.SemaphoreType.DMA((12, 2)),
            pltpu.SemaphoreType.DMA((3,)), pltpu.SemaphoreType.DMA((3,)),
        ],
        compiler_params=pltpu.CompilerParams(
            collective_id=0, has_side_effects=True, vmem_limit_bytes=54 * 1024 * 1024
        ),
    )(jacobian, right_side, scales, weights, aggregate_of)
    return (step * direction, right_side - step * image)


def solution(mesh):
    return jax.shard_map(
        functools.partial(shards, mesh.shape["cells"]),
        mesh=mesh,
        in_specs=(
            P(None, None, ("groups", "cells"), None, None),
            P(None, ("groups", "cells"), None, None),
            P(None, ("groups", "cells"), None, None),
            P(None, ("groups", "cells"), None, None),
            P(("groups", "cells"), None, None),
        ),
        out_specs=(
            P(None, ("groups", "cells"), None, None),
            P(None, ("groups", "cells"), None, None),
        ),
        check_vma=False,
    )
```

```python
import functools

import jax
import jax.numpy as jnp
from jax import lax
from jax.experimental import pallas as pl
from jax.experimental.pallas import tpu as pltpu
from jax.sharding import PartitionSpec as P

AY = 4
AX = 8
DAMPING = 2.0 / 3.0
LIFT = 1024.0
F32 = jnp.float32
BF16 = jnp.bfloat16


def split_rows(x):
    hi = x.astype(BF16)
    lo = (x - hi.astype(F32)).astype(BF16)
    return jnp.concatenate([hi, lo], axis=0)


def other_box(place, width):
    part = place % width
    own = place // width
    return jnp.where(part == 0, own - 1, jnp.where(part == width - 1, own + 1, -9))


def kernel(
    n, lz, gy, gx,
    jac_hbm, side_hbm, scal_hbm, wei_hbm, ids_hbm,
    dir_hbm, img_hbm, step_ref,
    jac, side, scal, wei, ids,
    pc, wd, rest, binv, zed, dout, iout,
    f1, f2, cf, lf, t3, pf, dr, c1, mh, mo, f2s, t3s, drs, mm, mmh, zz,
    mask, gidx, sx, sy, inv, shv,
    g0, g4, g9, g0s, g4s, g9s,
    lsem, osem, hs, hr, gs, gr,
):
    me = lax.axis_index("cells")
    has_low = me > 0
    has_high = me < n - 1
    low_id = jnp.maximum(me - 1, 0)
    high_id = jnp.minimum(me + 1, n - 1)
    top = lz - 1
    across = gx // AX
    half = gx // 2
    tiles = gy // 8

    barrier = pltpu.get_barrier_semaphore()

    @pl.loop(1, n)
    def _(step):
        pl.semaphore_signal(
            barrier, inc=1, device_id={"cells": lax.rem(me + step, n)},
            device_id_type=pl.DeviceIdType.MESH,
        )

    loads = []

    def load(src, dst):
        copy = pltpu.make_async_copy(src, dst, lsem.at[len(loads)])
        copy.start()
        loads.append(copy)
        return copy

    first_loads = [load(wei_hbm, wei), load(scal_hbm, scal)]
    first_loads += [load(jac_hbm.at[:, 3 * r], jac.at[:, 3 * r]) for r in range(3)]
    first_loads += [load(side_hbm, side)]
    ids_load = load(ids_hbm, ids)
    late_loads = [load(jac_hbm.at[:, e], jac.at[:, e]) for e in (1, 2, 4, 5, 7, 8)]

    k_row = lax.broadcasted_iota(jnp.int32, (gx, 128), 0)
    k_lane = lax.broadcasted_iota(jnp.int32, (gx, 128), 1) % across
    own = (k_row // AX == k_lane).astype(F32)
    oth = (other_box(k_row, AX) == k_lane).astype(F32)
    sx[0:gx, :] = own.astype(BF16)
    sx[gx:, :] = (oth - own).astype(BF16)
    m_row = lax.broadcasted_iota(jnp.int32, (128, 4 * gy), 0)
    m_col = lax.broadcasted_iota(jnp.int32, (128, 4 * gy), 1)
    box_row = 2 * ((m_row % 32) // 8) - 1 + m_row // 32
    grid_row = m_col % gy
    own = (grid_row // AY == box_row).astype(F32)
    oth = (other_box(grid_row, AY) == box_row).astype(F32)
    sy[...] = jnp.where((m_col // gy) % 2 == 0, own, oth - own).astype(BF16)

    zero = jnp.zeros((gy, gx), F32)

    @pl.when(jnp.logical_not(has_low))
    def _():
        for buf in (f1, f2, cf, lf, t3, pf):
            buf[0] = zero
        c1[1] = zero
        mh[1] = zero
        for c in range(3):
            dr[0, c] = zero
            mmh[1, c] = zero

    @pl.when(jnp.logical_not(has_high))
    def _():
        for buf in (f1, f2, cf, lf, t3, pf):
            buf[lz + 1] = zero
        c1[0] = zero
        mh[0] = zero
        for c in range(3):
            dr[lz + 1, c] = zero
            mmh[0, c] = zero

    def up_copy(e, src, dst):
        return pltpu.make_async_remote_copy(
            src_ref=src, dst_ref=dst, send_sem=hs.at[e, 0], recv_sem=hr.at[e, 0],
            device_id={"cells": high_id}, device_id_type=pl.DeviceIdType.MESH,
        )

    def down_copy(e, src, dst):
        return pltpu.make_async_remote_copy(
            src_ref=src, dst_ref=dst, send_sem=hs.at[e, 1], recv_sem=hr.at[e, 1],
            device_id={"cells": low_id}, device_id_type=pl.DeviceIdType.MESH,
        )

    pairs = []

    def exchange(up_src, up_dst, down_src, down_dst):
        e = len(pairs)
        up = up_copy(e, up_src, up_dst)
        down = down_copy(e, down_src, down_dst)
        pairs.append((up, down))

        @pl.when(has_high)
        def _():
            up.start()

        @pl.when(has_low)
        def _():
            down.start()

        def arrive():
            @pl.when(has_low)
            def _():
                up.wait_recv()

            @pl.when(has_high)
            def _():
                down.wait_recv()

        return arrive

    def halo(buf):
        return exchange(buf.at[lz], buf.at[0], buf.at[1], buf.at[lz + 1])

    groups = []

    def spread(e, src, slots):
        src_ref = src

        def copy(step):
            return pltpu.make_async_remote_copy(
                src_ref=src_ref, dst_ref=slots.at[me], send_sem=gs.at[e],
                recv_sem=gr.at[e], device_id={"cells": lax.rem(me + step, n)},
                device_id_type=pl.DeviceIdType.MESH,
            )

        @pl.loop(1, n)
        def _(step):
            copy(step).start()

        slots[me] = src[...]

        def arrive():
            pltpu.make_async_copy(
                slots.at[pl.ds(0, n - 1)], slots.at[pl.ds(0, n - 1)], gr.at[e]
            ).wait()

        def sent():
            pltpu.make_async_copy(
                slots.at[pl.ds(0, n - 1)], slots.at[pl.ds(0, n - 1)], gs.at[e]
            ).wait()

        groups.append(sent)
        return arrive

    y_at = lax.broadcasted_iota(jnp.int32, (gy, gx), 0)
    x_at = lax.broadcasted_iota(jnp.int32, (gy, gx), 1)
    in_grid = [y_at > 0, y_at < gy - 1, x_at > 0, x_at < gx - 1]

    def shifted(v, way):
        if way == 0:
            return pltpu.roll(v, 1, 0)
        if way == 1:
            return pltpu.roll(v, gy - 1, 0)
        if way == 2:
            return pltpu.roll(v, 1, 1)
        return pltpu.roll(v, gx - 1, 1)

    for copy in first_loads:
        copy.wait()

    def pressure_layer(z):
        ws = [wei[r, z] * scal[r, z] for r in range(3)]
        low_keep = jnp.where(jnp.logical_and(z == 0, me == 0), 0.0, 1.0)
        high_keep = jnp.where(jnp.logical_and(z == top, me == n - 1), 0.0, 1.0)
        for k in range(7):
            s = ws[0] * jac[k, 0, z].astype(F32)
            for r in range(1, 3):
                s = s + ws[r] * jac[k, 3 * r, z].astype(F32)
            if k == 1:
                s = s * low_keep
            if k == 2:
                s = s * high_keep
            if k >= 3:
                s = jnp.where(in_grid[k - 3], s, 0.0)
            pc[k, z] = s
            if k == 0:
                w = DAMPING / s
        rs = LIFT * (wei[0, z] * side[0, z] + wei[1, z] * side[1, z] + wei[2, z] * side[2, z])
        rest[z] = rs
        wd[z] = w
        f1[z + 1] = rs * w

    @pl.loop(0, 2)
    def _(i):
        pressure_layer(i * top)

    pl.semaphore_wait(barrier, n - 1)
    f1_in = halo(f1)

    @pl.loop(1, top)
    def _(z):
        pressure_layer(z)

    mo[0] = wd[0] * pc[1, 0]
    mo[1] = wd[top] * pc[2, top]
    m_in = exchange(mo.at[1], mh.at[1], mo.at[0], mh.at[0])

    def complete(below, buf):
        buf[1] = buf[1] - mo[0] * below[0]
        buf[lz] = buf[lz] - mo[1] * below[lz + 1]
        buf[0] = buf[0] - mh[1] * below[1]
        buf[lz + 1] = buf[lz + 1] - mh[0] * below[lz]

    def inner(buf, z):
        v = buf[z + 1]
        s = pc[0, z] * v
        for way in range(4):
            s = s + pc[3 + way, z] * shifted(v, way)
        if z > 0:
            s = s + pc[1, z] * buf[z]
        if z < top:
            s = s + pc[2, z] * buf[z + 2]
        return s

    for z in (0, top):
        f2[z + 1] = f1[z + 1] + wd[z] * (rest[z] - inner(f1, z))
    f2s[0] = f2[1]
    f2s[1] = f2[lz]
    f2_in = exchange(f2s.at[1], f2.at[0], f2s.at[0], f2.at[lz + 1])
    for z in range(1, top):
        f2[z + 1] = f1[z + 1] + wd[z] * (rest[z] - inner(f1, z))

    row_sum = []
    main = zero
    for z in range(lz):
        s = pc[0, z] + pc[3, z] + pc[4, z] + pc[5, z] + pc[6, z]
        if z > 0:
            s = s + pc[1, z]
        if z < top:
            s = s + pc[2, z]
        row_sum.append(s)
        main = main + s
        zed[0, z] = s

    def total(v):
        s = jnp.sum(v, axis=0, keepdims=True)
        return jnp.sum(s, axis=1, keepdims=True)

    g0s[0:1, :] = jnp.broadcast_to(total(main), (1, 128))
    g0s[1:2, :] = jnp.broadcast_to(total(pc[1, 0]), (1, 128))
    g0s[2:3, :] = jnp.broadcast_to(total(pc[2, top]), (1, 128))
    g0s[3:8, :] = jnp.zeros((5, 128), F32)
    g0_in = spread(0, g0s, g0)
    c_in = exchange(pc.at[2, top], c1.at[1], pc.at[1, 0], c1.at[0])

    ids_load.wait()
    for z in range(lz):
        a = ids[z]
        ro = (a // across != y_at // AY).astype(F32)
        co = (a % across != x_at // AX).astype(F32)
        mask[0, z] = ro
        mask[1, z] = co
        mask[2, z] = ro * co
        gidx[z] = jnp.clip(a - (2 * (y_at // 8) - 1) * across, 0, 127)

    def gathered(layers):
        t = zero
        sums = [zero, zero, zero]
        for z, v in layers:
            t = t + v
            for i in range(3):
                sums[i] = sums[i] + mask[i, z] * v
        return [t] + sums

    group_at = lax.broadcasted_iota(jnp.int32, (gy, 128), 1) // across

    def restrict(parts):
        t, ro, co, rc = parts
        stacked = jnp.concatenate(
            [jnp.concatenate([t, co], axis=1), jnp.concatenate([ro, rc], axis=1)], axis=0
        )
        out = jnp.dot(split_rows(stacked), sx[...], preferred_element_type=F32)
        out = out[: 2 * gy] + out[2 * gy :]
        out = jnp.dot(sy[...], split_rows(out), preferred_element_type=F32)
        res = out[0:gy]
        for g in range(1, 4):
            res = jnp.where(group_at == g, out[g * gy : (g + 1) * gy], res)
        return res

    def prolong(table, buf, z):
        for h in range(2):
            buf[z + 1, :, h * half : (h + 1) * half] = jnp.take_along_axis(
                table, gidx[z, :, h * half : (h + 1) * half], axis=1
            )

    def diag_layer(z):
        a = ids[z]
        s = pc[0, z]
        for way in range(4):
            s = s + jnp.where(shifted(a, way) == a, pc[3 + way, z], 0.0)
        if z > 0:
            s = s + jnp.where(ids[z - 1] == a, pc[1, z], 0.0)
        if z < top:
            s = s + jnp.where(ids[z + 1] == a, pc[2, z], 0.0)
        return s

    wdiag = DAMPING / restrict(gathered([(z, diag_layer(z)) for z in range(lz)]))

    for z in range(lz):
        for r in range(3):
            zz[r, z] = LIFT * side[r, z] / scal[r, z]

    f1_in()
    m_in()
    f2_in()
    complete(f1, f2)
    for z in range(lz):
        zed[1, z] = rest[z] - inner(f2, z)
    zed[1, 0] = zed[1, 0] - pc[1, 0] * f2[0]
    zed[1, top] = zed[1, top] - pc[2, top] * f2[lz + 1]
    rhs = restrict(gathered([(z, zed[1, z]) for z in range(lz)]))
    coarse_first = wdiag * rhs
    prolong(coarse_first, cf, 0)
    prolong(coarse_first, cf, top)
    cf_in = halo(cf)
    for z in range(1, top):
        prolong(coarse_first, cf, z)
    own_sum = zero
    for z in range(lz):
        q = zed[1, z] - inner(cf, z)
        zed[1, z] = q
        own_sum = own_sum + q
    c_in()
    lane = lax.broadcasted_iota(jnp.int32, (1, 128), 1)
    tile = jnp.where(lane == me, total(own_sum), 0.0)
    tile = tile - jnp.where(lane == me + 1, total(c1[0] * cf[lz]), 0.0)
    tile = tile - jnp.where(lane == me - 1, total(c1[1] * cf[1]), 0.0)
    g4s[...] = jnp.broadcast_to(tile, (8, 128))
    g4_in = spread(1, g4s, g4)

    g0_in()
    inv[0] = jnp.zeros((1, 128), F32)
    inv[n + 1] = jnp.zeros((1, 128), F32)
    previous_c = jnp.zeros((1, 128), F32)
    previous_d = jnp.zeros((1, 128), F32)
    for j in range(n):
        m, l, u = g0[j, 0:1, :], g0[j, 1:2, :], g0[j, 2:3, :]
        scale = 1.0 / (m - l * previous_c)
        previous_c = u * scale
        previous_d = (jnp.where(lane == j, 1.0, 0.0) - l * previous_d) * scale
        shv[j] = previous_c
        inv[j + 1] = previous_d
    for j in range(n - 2, -1, -1):
        inv[j + 1] = inv[j + 1] - shv[j] * inv[j + 2]

    row_part = restrict(gathered([(z, zed[0, z]) for z in range(lz)]))
    low_part = restrict(gathered([(0, pc[1, 0])]))
    high_part = restrict(gathered([(top, pc[2, top])]))

    cf_in()
    zed[1, 0] = zed[1, 0] - pc[1, 0] * cf[0]
    zed[1, top] = zed[1, top] - pc[2, top] * cf[lz + 1]
    rhs = restrict(gathered([(z, zed[1, z]) for z in range(lz)]))

    for copy in late_loads:
        copy.wait()

    @pl.loop(0, lz)
    def _(z):
        mat = [jac[0, e, z].astype(F32) for e in range(9)]
        co_aa = mat[4] * mat[8] - mat[5] * mat[7]
        co_ab = mat[5] * mat[6] - mat[3] * mat[8]
        co_ac = mat[3] * mat[7] - mat[4] * mat[6]
        det = 1.0 / (mat[0] * co_aa + mat[1] * co_ab + mat[2] * co_ac)
        binv[0, z] = co_aa * det
        binv[3, z] = co_ab * det
        binv[6, z] = co_ac * det
        binv[1, z] = (mat[2] * mat[7] - mat[1] * mat[8]) * det
        binv[4, z] = (mat[0] * mat[8] - mat[2] * mat[6]) * det
        binv[7, z] = (mat[1] * mat[6] - mat[0] * mat[7]) * det
        binv[2, z] = (mat[1] * mat[5] - mat[2] * mat[4]) * det
        binv[5, z] = (mat[2] * mat[3] - mat[0] * mat[5]) * det
        binv[8, z] = (mat[0] * mat[4] - mat[1] * mat[3]) * det

    for side_at, z, k in ((0, 0, 1), (1, top, 2)):
        for c in range(3):
            v = binv[3 * c, z] * jac[k, 0, z].astype(F32)
            for r in range(1, 3):
                v = v + binv[3 * c + r, z] * jac[k, 3 * r, z].astype(F32)
            mm[side_at, c] = v
    mm_in = exchange(mm.at[1], mmh.at[1], mm.at[0], mmh.at[0])

    g4_in()
    res = g4[0, 0:1, :]
    for j in range(1, n):
        res = res + g4[j, 0:1, :]

    def fix_of(row):
        return jnp.sum(inv[row] * res, axis=1, keepdims=True)

    fix_low, fix_own, fix_high = fix_of(me), fix_of(me + 1), fix_of(me + 2)
    coarse_third = (
        coarse_first
        + fix_own
        + wdiag * (rhs - fix_own * row_part - fix_low * low_part - fix_high * high_part)
    )
    prolong(coarse_third, lf, 0)
    prolong(coarse_third, lf, top)
    lf_in = halo(lf)
    for z in range(1, top):
        prolong(coarse_third, lf, z)
    for z in (0, top):
        t3[z + 1] = f2[z + 1] + lf[z + 1] - wd[z] * inner(lf, z)
    t3s[0] = t3[1]
    t3s[1] = t3[lz]
    t3_in = exchange(t3s.at[1], t3.at[0], t3s.at[0], t3.at[lz + 1])
    for z in range(1, top):
        t3[z + 1] = f2[z + 1] + lf[z + 1] - wd[z] * inner(lf, z)
    lf_in()
    t3_in()
    complete(lf, t3)
    for z in range(lz):
        pf[z + 1] = t3[z + 1] + wd[z] * (rest[z] - inner(t3, z))
    pf[1] = pf[1] - mo[0] * t3[0]
    pf[lz] = pf[lz] - mo[1] * t3[lz + 1]
    pf_in = halo(pf)

    def near_terms(v, way):
        return jnp.where(in_grid[way], shifted(v, way), 0.0)

    def section_layer(z):
        v = pf[z + 1]
        acc = [zz[r, z] for r in range(3)]
        for way in range(4):
            s = near_terms(v, way)
            for r in range(3):
                acc[r] = acc[r] - jac[3 + way, 3 * r, z].astype(F32) * s
        if z > 0:
            for r in range(3):
                acc[r] = acc[r] - jac[1, 3 * r, z].astype(F32) * pf[z]
        if z < top:
            for r in range(3):
                acc[r] = acc[r] - jac[2, 3 * r, z].astype(F32) * pf[z + 2]
        for r in range(3):
            zed[r, z] = acc[r]

    def solve_layer(z):
        v = [zed[r, z] for r in range(3)]
        for c in range(3):
            d = binv[3 * c, z] * v[0] + binv[3 * c + 1, z] * v[1] + binv[3 * c + 2, z] * v[2]
            dr[z + 1, c] = d

    section_layer(0)
    section_layer(top)
    solve_layer(0)
    solve_layer(top)
    for c in range(3):
        drs[0, c] = dr[1, c]
        drs[1, c] = dr[lz, c]
    dr_in = exchange(drs.at[1], dr.at[0], drs.at[0], dr.at[lz + 1])
    for z in range(1, top):
        section_layer(z)
    for z in range(1, top):
        solve_layer(z)

    def in_layer(z, acc):
        for c in range(3):
            v = dr[z + 1, c]
            for way in range(4):
                s = near_terms(v, way)
                for r in range(3):
                    acc[r] = acc[r] + jac[3 + way, 3 * r + c, z].astype(F32) * s
        return acc

    def from_layer(z, k, acc):
        for c in range(3):
            v = dr[z + 2 * k - 2, c]
            for r in range(3):
                acc[r] = acc[r] + jac[k, 3 * r + c, z].astype(F32) * v
        return acc

    def early(z):
        acc = [zed[r, z] for r in range(3)]
        if 0 < z < top:
            acc = in_layer(z, acc)
        if z > 1:
            acc = from_layer(z, 1, acc)
        if z < top - 1:
            acc = from_layer(z, 2, acc)
        for r in range(3):
            zed[r, z] = acc[r]

    for z in range(lz):
        early(z)

    mm_in()
    pf_in()
    for r in range(3):
        zed[r, 0] = zed[r, 0] - jac[1, 3 * r, 0].astype(F32) * pf[0]
        zed[r, top] = zed[r, top] - jac[2, 3 * r, top].astype(F32) * pf[lz + 1]
    for c in range(3):
        dr[1, c] = dr[1, c] - mm[0, c] * pf[0]
        dr[lz, c] = dr[lz, c] - mm[1, c] * pf[lz + 1]
    def late(z):
        acc = [zed[r, z] for r in range(3)]
        if z == 0 or z == top:
            acc = in_layer(z, acc)
        if z == 1:
            acc = from_layer(z, 1, acc)
        if z == top - 1:
            acc = from_layer(z, 2, acc)
        for r in range(3):
            zed[r, z] = acc[r]

    for z in range(lz):
        for c in range(3):
            dout[c, z] = dr[z + 1, c]
    dir_out = pltpu.make_async_copy(dout, dir_hbm, osem.at[0])
    dir_out.start()
    for z in range(lz):
        late(z)
    dr_in()
    for c in range(3):
        low = dr[0, c] - mmh[1, c] * pf[1]
        high = dr[lz + 1, c] - mmh[0, c] * pf[lz]
        for r in range(3):
            zed[r, 0] = zed[r, 0] + jac[1, 3 * r + c, 0].astype(F32) * low
            zed[r, top] = zed[r, top] + jac[2, 3 * r + c, top].astype(F32) * high
    s1, s2, s3 = zero, zero, zero
    for z in range(lz):
        for r in range(3):
            b = side[r, z]
            v = scal[r, z] * zed[r, z]
            iout[r, z] = v
            s1 = s1 + b * b
            s2 = s2 + v * (LIFT * b)
            s3 = s3 + v * v

    img_out = pltpu.make_async_copy(iout, img_hbm, osem.at[1])
    img_out.start()

    def lanes(v):
        s = v[:, :half] + v[:, half:]
        return jnp.sum(s, axis=0, keepdims=True)

    g9s[0:1, :] = lanes(s1)
    g9s[1:2, :] = lanes(s2)
    g9s[2:3, :] = lanes(s3)
    g9s[3:8, :] = jnp.zeros((5, 128), F32)
    g9_in = spread(2, g9s, g9)
    g9_in()
    tot = g9[0]
    for j in range(1, n):
        tot = tot + g9[j]
    tot = jnp.sum(tot, axis=1, keepdims=True)
    along = tot[1:2] / (LIFT * (tot[0:1] + 1e-6))
    step = tot[1:2] / (LIFT * (tot[2:3] - 1e-6 * along * along))
    step_ref[...] = jnp.broadcast_to(step, (gy, gx))

    for up, down in pairs:
        @pl.when(has_high)
        def _(up=up):
            up.wait_send()

        @pl.when(has_low)
        def _(down=down):
            down.wait_send()

    for sent in groups:
        sent()
    dir_out.wait()
    img_out.wait()


def shards(n, jacobian, right_side, scales, weights, aggregate_of):
    lz, gy, gx = aggregate_of.shape
    field = (lz, gy, gx)
    border = (lz + 2, gy, gx)
    vm = lambda shape, dtype=F32: pltpu.VMEM(shape, dtype)
    any_spec = pl.BlockSpec(memory_space=pl.ANY)
    vmem_spec = pl.BlockSpec(memory_space=pltpu.VMEM)
    direction, image, step = pl.pallas_call(
        functools.partial(kernel, n, lz, gy, gx),
        out_shape=(
            jax.ShapeDtypeStruct((3,) + field, F32),
            jax.ShapeDtypeStruct((3,) + field, F32),
            jax.ShapeDtypeStruct((gy, gx), F32),
        ),
        in_specs=[pl.BlockSpec(memory_space=pltpu.HBM)] * 5,
        out_specs=(any_spec, any_spec, vmem_spec),
        scratch_shapes=[
            vm((7, 9) + field, BF16), vm((3,) + field), vm((3,) + field), vm((3,) + field),
            vm(field, jnp.int32),
            vm((7,) + field), vm(field), vm(field), vm((9,) + field), vm((3,) + field),
            vm((3,) + field), vm((3,) + field),
            vm(border), vm(border), vm(border), vm(border), vm(border), vm(border),
            vm((lz + 2, 3, gy, gx)), vm((2, gy, gx)), vm((2, gy, gx)), vm((2, gy, gx)),
            vm((2, gy, gx)), vm((2, gy, gx)), vm((2, 3, gy, gx)), vm((2, 3, gy, gx)),
            vm((2, 3, gy, gx)), vm((3,) + field),
            vm((3,) + field), vm(field, jnp.int32), vm((2 * gx, 128), BF16),
            vm((128, 4 * gy), BF16), vm((n + 2, 1, 128)), vm((n, 1, 128)),
            vm((n, 8, 128)), vm((n, 8, 128)), vm((n, 8, 128)),
            vm((8, 128)), vm((8, 128)), vm((8, 128)),
            pltpu.SemaphoreType.DMA((16,)), pltpu.SemaphoreType.DMA((2,)),
            pltpu.SemaphoreType.DMA((12, 2)), pltpu.SemaphoreType.DMA((12, 2)),
            pltpu.SemaphoreType.DMA((3,)), pltpu.SemaphoreType.DMA((3,)),
        ],
        compiler_params=pltpu.CompilerParams(
            collective_id=0, has_side_effects=True, vmem_limit_bytes=60 * 1024 * 1024
        ),
    )(jacobian, right_side, scales, weights, aggregate_of)
    return (step * direction, right_side - step * image)


def solution(mesh):
    return jax.shard_map(
        functools.partial(shards, mesh.shape["cells"]),
        mesh=mesh,
        in_specs=(
            P(None, None, ("groups", "cells"), None, None),
            P(None, ("groups", "cells"), None, None),
            P(None, ("groups", "cells"), None, None),
            P(None, ("groups", "cells"), None, None),
            P(("groups", "cells"), None, None),
        ),
        out_specs=(
            P(None, ("groups", "cells"), None, None),
            P(None, ("groups", "cells"), None, None),
        ),
        check_vma=False,
    )
```

```python
import functools

import jax
import jax.numpy as jnp
from jax import lax
from jax.experimental import pallas as pl
from jax.experimental.pallas import tpu as pltpu
from jax.sharding import PartitionSpec as P

AY = 4
AX = 8
DAMPING = 2.0 / 3.0
LIFT = 1024.0
F32 = jnp.float32
BF16 = jnp.bfloat16


def split_rows(x):
    hi = x.astype(BF16)
    lo = (x - hi.astype(F32)).astype(BF16)
    return jnp.concatenate([hi, lo], axis=0)


def other_box(place, width):
    part = place % width
    own = place // width
    return jnp.where(part == 0, own - 1, jnp.where(part == width - 1, own + 1, -9))


def kernel(
    n, lz, gy, gx,
    jac_hbm, side_hbm, scal_hbm, wei_hbm, ids_hbm,
    dir_hbm, img_hbm, step_ref,
    jac, side, scal, wei, ids,
    pc, wd, rest, binv, zed, dout, iout,
    f1, f2, cf, lf, t3, pf, dr, c1, mh, mo, f2s, t3s, drs, mm, mmh, zz,
    mask, gidx, sx, sy, inv, shv,
    g0, g4, g9, g0s, g4s, g9s,
    lsem, osem, hs, hr, gs, gr,
):
    me = lax.axis_index("cells")
    has_low = me > 0
    has_high = me < n - 1
    low_id = jnp.maximum(me - 1, 0)
    high_id = jnp.minimum(me + 1, n - 1)
    top = lz - 1
    across = gx // AX
    half = gx // 2
    tiles = gy // 8

    barrier = pltpu.get_barrier_semaphore()

    @pl.loop(1, n)
    def _(step):
        pl.semaphore_signal(
            barrier, inc=1, device_id={"cells": lax.rem(me + step, n)},
            device_id_type=pl.DeviceIdType.MESH,
        )

    loads = []

    def load(src, dst):
        copy = pltpu.make_async_copy(src, dst, lsem.at[len(loads)])
        copy.start()
        loads.append(copy)
        return copy

    first_loads = [load(wei_hbm, wei), load(scal_hbm, scal)]
    first_loads += [load(jac_hbm.at[:, 3 * r], jac.at[:, 3 * r]) for r in range(3)]
    first_loads += [load(side_hbm, side)]
    ids_load = load(ids_hbm, ids)
    late_loads = [load(jac_hbm.at[:, e], jac.at[:, e]) for e in (1, 2, 4, 5, 7, 8)]

    k_row = lax.broadcasted_iota(jnp.int32, (gx, 128), 0)
    k_lane = lax.broadcasted_iota(jnp.int32, (gx, 128), 1) % across
    own = (k_row // AX == k_lane).astype(F32)
    oth = (other_box(k_row, AX) == k_lane).astype(F32)
    sx[0:gx, :] = own.astype(BF16)
    sx[gx:, :] = (oth - own).astype(BF16)
    m_row = lax.broadcasted_iota(jnp.int32, (128, 4 * gy), 0)
    m_col = lax.broadcasted_iota(jnp.int32, (128, 4 * gy), 1)
    box_row = 2 * ((m_row % 32) // 8) - 1 + m_row // 32
    grid_row = m_col % gy
    own = (grid_row // AY == box_row).astype(F32)
    oth = (other_box(grid_row, AY) == box_row).astype(F32)
    sy[...] = jnp.where((m_col // gy) % 2 == 0, own, oth - own).astype(BF16)

    zero = jnp.zeros((gy, gx), F32)

    @pl.when(jnp.logical_not(has_low))
    def _():
        for buf in (f1, f2, cf, lf, t3, pf):
            buf[0] = zero
        c1[1] = zero
        mh[1] = zero
        for c in range(3):
            dr[0, c] = zero
            mmh[1, c] = zero

    @pl.when(jnp.logical_not(has_high))
    def _():
        for buf in (f1, f2, cf, lf, t3, pf):
            buf[lz + 1] = zero
        c1[0] = zero
        mh[0] = zero
        for c in range(3):
            dr[lz + 1, c] = zero
            mmh[0, c] = zero

    def up_copy(e, src, dst):
        return pltpu.make_async_remote_copy(
            src_ref=src, dst_ref=dst, send_sem=hs.at[e, 0], recv_sem=hr.at[e, 0],
            device_id={"cells": high_id}, device_id_type=pl.DeviceIdType.MESH,
        )

    def down_copy(e, src, dst):
        return pltpu.make_async_remote_copy(
            src_ref=src, dst_ref=dst, send_sem=hs.at[e, 1], recv_sem=hr.at[e, 1],
            device_id={"cells": low_id}, device_id_type=pl.DeviceIdType.MESH,
        )

    pairs = []

    def exchange(up_src, up_dst, down_src, down_dst):
        e = len(pairs)
        up = up_copy(e, up_src, up_dst)
        down = down_copy(e, down_src, down_dst)
        pairs.append((up, down))

        @pl.when(has_high)
        def _():
            up.start()

        @pl.when(has_low)
        def _():
            down.start()

        def arrive():
            @pl.when(has_low)
            def _():
                up.wait_recv()

            @pl.when(has_high)
            def _():
                down.wait_recv()

        return arrive

    def halo(buf):
        return exchange(buf.at[lz], buf.at[0], buf.at[1], buf.at[lz + 1])

    groups = []

    def spread(e, src, slots):
        src_ref = src

        def copy(step):
            return pltpu.make_async_remote_copy(
                src_ref=src_ref, dst_ref=slots.at[me], send_sem=gs.at[e],
                recv_sem=gr.at[e], device_id={"cells": lax.rem(me + step, n)},
                device_id_type=pl.DeviceIdType.MESH,
            )

        for step in range(1, n):
            copy(step).start()

        slots[me] = src[...]

        def arrive():
            pltpu.make_async_copy(
                slots.at[pl.ds(0, n - 1)], slots.at[pl.ds(0, n - 1)], gr.at[e]
            ).wait()

        def sent():
            pltpu.make_async_copy(
                slots.at[pl.ds(0, n - 1)], slots.at[pl.ds(0, n - 1)], gs.at[e]
            ).wait()

        groups.append(sent)
        return arrive

    y_at = lax.broadcasted_iota(jnp.int32, (gy, gx), 0)
    x_at = lax.broadcasted_iota(jnp.int32, (gy, gx), 1)
    in_grid = [y_at > 0, y_at < gy - 1, x_at > 0, x_at < gx - 1]

    def shifted(v, way):
        if way == 0:
            return pltpu.roll(v, 1, 0)
        if way == 1:
            return pltpu.roll(v, gy - 1, 0)
        if way == 2:
            return pltpu.roll(v, 1, 1)
        return pltpu.roll(v, gx - 1, 1)

    for copy in first_loads:
        copy.wait()

    def pressure_layer(z):
        ws = [wei[r, z] * scal[r, z] for r in range(3)]
        low_keep = jnp.where(jnp.logical_and(z == 0, me == 0), 0.0, 1.0)
        high_keep = jnp.where(jnp.logical_and(z == top, me == n - 1), 0.0, 1.0)
        for k in range(7):
            s = ws[0] * jac[k, 0, z].astype(F32)
            for r in range(1, 3):
                s = s + ws[r] * jac[k, 3 * r, z].astype(F32)
            if k == 1:
                s = s * low_keep
            if k == 2:
                s = s * high_keep
            if k >= 3:
                s = jnp.where(in_grid[k - 3], s, 0.0)
            pc[k, z] = s
            if k == 0:
                w = DAMPING / s
        rs = LIFT * (wei[0, z] * side[0, z] + wei[1, z] * side[1, z] + wei[2, z] * side[2, z])
        rest[z] = rs
        wd[z] = w
        f1[z + 1] = rs * w

    @pl.loop(0, 2)
    def _(i):
        pressure_layer(i * top)

    pl.semaphore_wait(barrier, n - 1)
    f1_in = halo(f1)

    @pl.loop(1, top)
    def _(z):
        pressure_layer(z)

    mo[0] = wd[0] * pc[1, 0]
    mo[1] = wd[top] * pc[2, top]
    m_in = exchange(mo.at[1], mh.at[1], mo.at[0], mh.at[0])

    def complete(below, buf):
        buf[1] = buf[1] - mo[0] * below[0]
        buf[lz] = buf[lz] - mo[1] * below[lz + 1]
        buf[0] = buf[0] - mh[1] * below[1]
        buf[lz + 1] = buf[lz + 1] - mh[0] * below[lz]

    def inner(buf, z):
        v = buf[z + 1]
        s = pc[0, z] * v
        for way in range(4):
            s = s + pc[3 + way, z] * shifted(v, way)
        if z > 0:
            s = s + pc[1, z] * buf[z]
        if z < top:
            s = s + pc[2, z] * buf[z + 2]
        return s

    for z in (0, top):
        f2[z + 1] = f1[z + 1] + wd[z] * (rest[z] - inner(f1, z))
    f2s[0] = f2[1]
    f2s[1] = f2[lz]
    f2_in = exchange(f2s.at[1], f2.at[0], f2s.at[0], f2.at[lz + 1])
    for z in range(1, top):
        f2[z + 1] = f1[z + 1] + wd[z] * (rest[z] - inner(f1, z))

    row_sum = []
    main = zero
    for z in range(lz):
        s = pc[0, z] + pc[3, z] + pc[4, z] + pc[5, z] + pc[6, z]
        if z > 0:
            s = s + pc[1, z]
        if z < top:
            s = s + pc[2, z]
        row_sum.append(s)
        main = main + s
        zed[0, z] = s

    def total(v):
        s = jnp.sum(v, axis=0, keepdims=True)
        return jnp.sum(s, axis=1, keepdims=True)

    g0s[0:1, :] = jnp.broadcast_to(total(main), (1, 128))
    g0s[1:2, :] = jnp.broadcast_to(total(pc[1, 0]), (1, 128))
    g0s[2:3, :] = jnp.broadcast_to(total(pc[2, top]), (1, 128))
    g0s[3:8, :] = jnp.zeros((5, 128), F32)
    g0_in = spread(0, g0s, g0)
    c_in = exchange(pc.at[2, top], c1.at[1], pc.at[1, 0], c1.at[0])

    ids_load.wait()
    for z in range(lz):
        a = ids[z]
        ro = (a // across != y_at // AY).astype(F32)
        co = (a % across != x_at // AX).astype(F32)
        mask[0, z] = ro
        mask[1, z] = co
        mask[2, z] = ro * co
        gidx[z] = jnp.clip(a - (2 * (y_at // 8) - 1) * across, 0, 127)

    def gathered(layers):
        t = zero
        sums = [zero, zero, zero]
        for z, v in layers:
            t = t + v
            for i in range(3):
                sums[i] = sums[i] + mask[i, z] * v
        return [t] + sums

    group_at = lax.broadcasted_iota(jnp.int32, (gy, 128), 1) // across

    def restrict(parts):
        t, ro, co, rc = parts
        stacked = jnp.concatenate(
            [jnp.concatenate([t, co], axis=1), jnp.concatenate([ro, rc], axis=1)], axis=0
        )
        out = jnp.dot(split_rows(stacked), sx[...], preferred_element_type=F32)
        out = out[: 2 * gy] + out[2 * gy :]
        out = jnp.dot(sy[...], split_rows(out), preferred_element_type=F32)
        res = out[0:gy]
        for g in range(1, 4):
            res = jnp.where(group_at == g, out[g * gy : (g + 1) * gy], res)
        return res

    def prolong(table, buf, z):
        for h in range(2):
            buf[z + 1, :, h * half : (h + 1) * half] = jnp.take_along_axis(
                table, gidx[z, :, h * half : (h + 1) * half], axis=1
            )

    def diag_layer(z):
        a = ids[z]
        s = pc[0, z]
        for way in range(4):
            s = s + jnp.where(shifted(a, way) == a, pc[3 + way, z], 0.0)
        if z > 0:
            s = s + jnp.where(ids[z - 1] == a, pc[1, z], 0.0)
        if z < top:
            s = s + jnp.where(ids[z + 1] == a, pc[2, z], 0.0)
        return s

    wdiag = DAMPING / restrict(gathered([(z, diag_layer(z)) for z in range(lz)]))

    for z in range(lz):
        for r in range(3):
            zz[r, z] = LIFT * side[r, z] / scal[r, z]

    for z in range(lz):
        s = pc[0, z]
        for way in range(4):
            s = s + shifted(pc[3 + way, z], way ^ 1)
        if z < top:
            s = s + pc[1, z + 1]
        if z > 0:
            s = s + pc[2, z - 1]
        zed[2, z] = s

    f1_in()
    m_in()
    f2_in()
    complete(f1, f2)
    for z in range(lz):
        zed[1, z] = rest[z] - inner(f2, z)
    zed[1, 0] = zed[1, 0] - pc[1, 0] * f2[0]
    zed[1, top] = zed[1, top] - pc[2, top] * f2[lz + 1]
    rhs = restrict(gathered([(z, zed[1, z]) for z in range(lz)]))
    coarse_first = wdiag * rhs
    prolong(coarse_first, cf, 0)
    prolong(coarse_first, cf, top)
    cf_in = halo(cf)
    for z in range(1, top):
        prolong(coarse_first, cf, z)
    own_sum = zero
    for z in range(lz):
        own_sum = own_sum + (zed[1, z] - zed[2, z] * cf[z + 1])
    c_in()
    lane = lax.broadcasted_iota(jnp.int32, (1, 128), 1)
    tile = jnp.where(lane == me, total(own_sum), 0.0)
    tile = tile - jnp.where(lane == me + 1, total(c1[0] * cf[lz]), 0.0)
    tile = tile - jnp.where(lane == me - 1, total(c1[1] * cf[1]), 0.0)
    g4s[...] = jnp.broadcast_to(tile, (8, 128))
    g4_in = spread(1, g4s, g4)
    for z in range(lz):
        zed[1, z] = zed[1, z] - inner(cf, z)

    g0_in()
    inv[0] = jnp.zeros((1, 128), F32)
    inv[n + 1] = jnp.zeros((1, 128), F32)
    previous_c = jnp.zeros((1, 128), F32)
    previous_d = jnp.zeros((1, 128), F32)
    for j in range(n):
        m, l, u = g0[j, 0:1, :], g0[j, 1:2, :], g0[j, 2:3, :]
        scale = 1.0 / (m - l * previous_c)
        previous_c = u * scale
        previous_d = (jnp.where(lane == j, 1.0, 0.0) - l * previous_d) * scale
        shv[j] = previous_c
        inv[j + 1] = previous_d
    for j in range(n - 2, -1, -1):
        inv[j + 1] = inv[j + 1] - shv[j] * inv[j + 2]

    row_part = restrict(gathered([(z, zed[0, z]) for z in range(lz)]))
    low_part = restrict(gathered([(0, pc[1, 0])]))
    high_part = restrict(gathered([(top, pc[2, top])]))

    cf_in()
    zed[1, 0] = zed[1, 0] - pc[1, 0] * cf[0]
    zed[1, top] = zed[1, top] - pc[2, top] * cf[lz + 1]
    rhs = restrict(gathered([(z, zed[1, z]) for z in range(lz)]))

    for copy in late_loads:
        copy.wait()

    @pl.loop(0, lz)
    def _(z):
        mat = [jac[0, e, z].astype(F32) for e in range(9)]
        co_aa = mat[4] * mat[8] - mat[5] * mat[7]
        co_ab = mat[5] * mat[6] - mat[3] * mat[8]
        co_ac = mat[3] * mat[7] - mat[4] * mat[6]
        det = 1.0 / (mat[0] * co_aa + mat[1] * co_ab + mat[2] * co_ac)
        binv[0, z] = co_aa * det
        binv[3, z] = co_ab * det
        binv[6, z] = co_ac * det
        binv[1, z] = (mat[2] * mat[7] - mat[1] * mat[8]) * det
        binv[4, z] = (mat[0] * mat[8] - mat[2] * mat[6]) * det
        binv[7, z] = (mat[1] * mat[6] - mat[0] * mat[7]) * det
        binv[2, z] = (mat[1] * mat[5] - mat[2] * mat[4]) * det
        binv[5, z] = (mat[2] * mat[3] - mat[0] * mat[5]) * det
        binv[8, z] = (mat[0] * mat[4] - mat[1] * mat[3]) * det

    for side_at, z, k in ((0, 0, 1), (1, top, 2)):
        for c in range(3):
            v = binv[3 * c, z] * jac[k, 0, z].astype(F32)
            for r in range(1, 3):
                v = v + binv[3 * c + r, z] * jac[k, 3 * r, z].astype(F32)
            mm[side_at, c] = v
    mm_in = exchange(mm.at[1], mmh.at[1], mm.at[0], mmh.at[0])

    g4_in()
    res = g4[0, 0:1, :]
    for j in range(1, n):
        res = res + g4[j, 0:1, :]

    def fix_of(row):
        return jnp.sum(inv[row] * res, axis=1, keepdims=True)

    fix_low, fix_own, fix_high = fix_of(me), fix_of(me + 1), fix_of(me + 2)
    coarse_third = (
        coarse_first
        + fix_own
        + wdiag * (rhs - fix_own * row_part - fix_low * low_part - fix_high * high_part)
    )
    prolong(coarse_third, lf, 0)
    prolong(coarse_third, lf, top)
    lf_in = halo(lf)
    for z in range(1, top):
        prolong(coarse_third, lf, z)
    for z in (0, top):
        t3[z + 1] = f2[z + 1] + lf[z + 1] - wd[z] * inner(lf, z)
    t3s[0] = t3[1]
    t3s[1] = t3[lz]
    t3_in = exchange(t3s.at[1], t3.at[0], t3s.at[0], t3.at[lz + 1])
    for z in range(1, top):
        t3[z + 1] = f2[z + 1] + lf[z + 1] - wd[z] * inner(lf, z)
    lf_in()
    t3_in()
    complete(lf, t3)
    for z in range(lz):
        pf[z + 1] = t3[z + 1] + wd[z] * (rest[z] - inner(t3, z))
    pf[1] = pf[1] - mo[0] * t3[0]
    pf[lz] = pf[lz] - mo[1] * t3[lz + 1]
    pf_in = halo(pf)

    def near_terms(v, way):
        return jnp.where(in_grid[way], shifted(v, way), 0.0)

    def section_layer(z):
        v = pf[z + 1]
        acc = [zz[r, z] for r in range(3)]
        for way in range(4):
            s = near_terms(v, way)
            for r in range(3):
                acc[r] = acc[r] - jac[3 + way, 3 * r, z].astype(F32) * s
        if z > 0:
            for r in range(3):
                acc[r] = acc[r] - jac[1, 3 * r, z].astype(F32) * pf[z]
        if z < top:
            for r in range(3):
                acc[r] = acc[r] - jac[2, 3 * r, z].astype(F32) * pf[z + 2]
        for r in range(3):
            zed[r, z] = acc[r]

    def solve_layer(z):
        v = [zed[r, z] for r in range(3)]
        for c in range(3):
            d = binv[3 * c, z] * v[0] + binv[3 * c + 1, z] * v[1] + binv[3 * c + 2, z] * v[2]
            dr[z + 1, c] = d

    section_layer(0)
    section_layer(top)
    solve_layer(0)
    solve_layer(top)
    for c in range(3):
        drs[0, c] = dr[1, c]
        drs[1, c] = dr[lz, c]
    dr_in = exchange(drs.at[1], dr.at[0], drs.at[0], dr.at[lz + 1])
    for z in range(1, top):
        section_layer(z)
    for z in range(1, top):
        solve_layer(z)

    def in_layer(z, acc):
        for c in range(3):
            v = dr[z + 1, c]
            for way in range(4):
                s = near_terms(v, way)
                for r in range(3):
                    acc[r] = acc[r] + jac[3 + way, 3 * r + c, z].astype(F32) * s
        return acc

    def from_layer(z, k, acc):
        for c in range(3):
            v = dr[z + 2 * k - 2, c]
            for r in range(3):
                acc[r] = acc[r] + jac[k, 3 * r + c, z].astype(F32) * v
        return acc

    def early(z):
        acc = [zed[r, z] for r in range(3)]
        if 0 < z < top:
            acc = in_layer(z, acc)
        if z > 1:
            acc = from_layer(z, 1, acc)
        if z < top - 1:
            acc = from_layer(z, 2, acc)
        for r in range(3):
            zed[r, z] = acc[r]

    for z in range(lz):
        early(z)

    mm_in()
    pf_in()
    for r in range(3):
        zed[r, 0] = zed[r, 0] - jac[1, 3 * r, 0].astype(F32) * pf[0]
        zed[r, top] = zed[r, top] - jac[2, 3 * r, top].astype(F32) * pf[lz + 1]
    for c in range(3):
        dr[1, c] = dr[1, c] - mm[0, c] * pf[0]
        dr[lz, c] = dr[lz, c] - mm[1, c] * pf[lz + 1]
    def late(z):
        acc = [zed[r, z] for r in range(3)]
        if z == 0 or z == top:
            acc = in_layer(z, acc)
        if z == 1:
            acc = from_layer(z, 1, acc)
        if z == top - 1:
            acc = from_layer(z, 2, acc)
        for r in range(3):
            zed[r, z] = acc[r]

    for z in range(lz):
        for c in range(3):
            dout[c, z] = dr[z + 1, c]
    dir_out = pltpu.make_async_copy(dout, dir_hbm, osem.at[0])
    dir_out.start()
    for z in range(lz):
        late(z)
    dr_in()
    for c in range(3):
        low = dr[0, c] - mmh[1, c] * pf[1]
        high = dr[lz + 1, c] - mmh[0, c] * pf[lz]
        for r in range(3):
            zed[r, 0] = zed[r, 0] + jac[1, 3 * r + c, 0].astype(F32) * low
            zed[r, top] = zed[r, top] + jac[2, 3 * r + c, top].astype(F32) * high
    s1, s2, s3 = zero, zero, zero
    for z in range(lz):
        for r in range(3):
            b = side[r, z]
            v = scal[r, z] * zed[r, z]
            iout[r, z] = v
            s1 = s1 + b * b
            s2 = s2 + v * (LIFT * b)
            s3 = s3 + v * v

    img_out = pltpu.make_async_copy(iout, img_hbm, osem.at[1])
    img_out.start()

    def lanes(v):
        s = v[:, :half] + v[:, half:]
        return jnp.sum(s, axis=0, keepdims=True)

    g9s[0:1, :] = lanes(s1)
    g9s[1:2, :] = lanes(s2)
    g9s[2:3, :] = lanes(s3)
    g9s[3:8, :] = jnp.zeros((5, 128), F32)
    g9_in = spread(2, g9s, g9)
    g9_in()
    tot = g9[0]
    for j in range(1, n):
        tot = tot + g9[j]
    tot = jnp.sum(tot, axis=1, keepdims=True)
    along = tot[1:2] / (LIFT * (tot[0:1] + 1e-6))
    step = tot[1:2] / (LIFT * (tot[2:3] - 1e-6 * along * along))
    step_ref[...] = jnp.broadcast_to(step, (gy, gx))

    for up, down in pairs:
        @pl.when(has_high)
        def _(up=up):
            up.wait_send()

        @pl.when(has_low)
        def _(down=down):
            down.wait_send()

    for sent in groups:
        sent()
    dir_out.wait()
    img_out.wait()


def shards(n, jacobian, right_side, scales, weights, aggregate_of):
    lz, gy, gx = aggregate_of.shape
    field = (lz, gy, gx)
    border = (lz + 2, gy, gx)
    vm = lambda shape, dtype=F32: pltpu.VMEM(shape, dtype)
    any_spec = pl.BlockSpec(memory_space=pl.ANY)
    vmem_spec = pl.BlockSpec(memory_space=pltpu.VMEM)
    direction, image, step = pl.pallas_call(
        functools.partial(kernel, n, lz, gy, gx),
        out_shape=(
            jax.ShapeDtypeStruct((3,) + field, F32),
            jax.ShapeDtypeStruct((3,) + field, F32),
            jax.ShapeDtypeStruct((gy, gx), F32),
        ),
        in_specs=[pl.BlockSpec(memory_space=pltpu.HBM)] * 5,
        out_specs=(any_spec, any_spec, vmem_spec),
        scratch_shapes=[
            vm((7, 9) + field, BF16), vm((3,) + field), vm((3,) + field), vm((3,) + field),
            vm(field, jnp.int32),
            vm((7,) + field), vm(field), vm(field), vm((9,) + field), vm((3,) + field),
            vm((3,) + field), vm((3,) + field),
            vm(border), vm(border), vm(border), vm(border), vm(border), vm(border),
            vm((lz + 2, 3, gy, gx)), vm((2, gy, gx)), vm((2, gy, gx)), vm((2, gy, gx)),
            vm((2, gy, gx)), vm((2, gy, gx)), vm((2, 3, gy, gx)), vm((2, 3, gy, gx)),
            vm((2, 3, gy, gx)), vm((3,) + field),
            vm((3,) + field), vm(field, jnp.int32), vm((2 * gx, 128), BF16),
            vm((128, 4 * gy), BF16), vm((n + 2, 1, 128)), vm((n, 1, 128)),
            vm((n, 8, 128)), vm((n, 8, 128)), vm((n, 8, 128)),
            vm((8, 128)), vm((8, 128)), vm((8, 128)),
            pltpu.SemaphoreType.DMA((16,)), pltpu.SemaphoreType.DMA((2,)),
            pltpu.SemaphoreType.DMA((12, 2)), pltpu.SemaphoreType.DMA((12, 2)),
            pltpu.SemaphoreType.DMA((3,)), pltpu.SemaphoreType.DMA((3,)),
        ],
        compiler_params=pltpu.CompilerParams(
            collective_id=0, has_side_effects=True, vmem_limit_bytes=60 * 1024 * 1024
        ),
    )(jacobian, right_side, scales, weights, aggregate_of)
    return (step * direction, right_side - step * image)


def solution(mesh):
    return jax.shard_map(
        functools.partial(shards, mesh.shape["cells"]),
        mesh=mesh,
        in_specs=(
            P(None, None, ("groups", "cells"), None, None),
            P(None, ("groups", "cells"), None, None),
            P(None, ("groups", "cells"), None, None),
            P(None, ("groups", "cells"), None, None),
            P(("groups", "cells"), None, None),
        ),
        out_specs=(
            P(None, ("groups", "cells"), None, None),
            P(None, ("groups", "cells"), None, None),
        ),
        check_vma=False,
    )
```
